32 devices in a mesh: row: 8 (over z, x), col: 2 (over y), rep: 2 (over core).
Axes of the slice: x: 2, y: 2, z: 4, core: 2. Of those that a mesh axis runs over, the one named last changes fastest.
Arguments:
- adj_tiles: float32 [8, 2, 4, 512, 512], P('row', 'col'), may hold values from -0.25 to 0.25
- tile_rows: int32 [8, 2, 4], P('row', 'col'), may hold values from 0 to 1
- tile_cols: int32 [8, 2, 4], P('row', 'col'), may hold values from 0 to 7
- tile_counts: int32 [8, 2], P('row', 'col'), may hold values from 1 to 4, as said below
- features_t: float32 [128, 8192], P('rep', ('row', 'col')), may hold values from -6 to 6
- weight: float32 [128, 128], P('rep'), may hold values from -0.5 to 0.5
- bias_vec: float32 [128], replicated, may hold values from -3 to 3
- cotangent: float32 [8192, 128], P(('row', 'col', 'rep')), may hold values from -0.02 to 0.02
Outputs:
- output: float32 [8192, 128], P(('row', 'col', 'rep'))
- grad_weight: float32 [128, 128], P('rep')
- grad_bias: float32 [128], replicated
The draws below stay inside these ranges and needn't reach their ends.
Inputs may be any that keep to these rules, and one draw needn't show every extreme that they name: `tile_counts`: the number of live slots of each cell; some cell has all 4 slots live. `tile_rows`: block row of a slot inside its row group; dead slots hold arbitrary values. `tile_cols`: block column of a slot inside its column group; dead slots hold arbitrary values.
All inputs are finite; a program needn't handle non-finite values.
Results may differ from the reference program's by a relative error of at most 0.0001.
Values sent between devices are 32-bit elements; how exact they have to be, the bound alone decides.
No kernel may reach another device: no remote copies, remote signals or barrier semaphores. Data moves between devices by JAX's collectives and lax.ppermute only.
A program may use at most 64 MiB of HBM per device.

```python
import jax
import jax.numpy as jnp
from jax import lax

F = 128
BLOCK = 512
TILES_DEV = 4
NODES = 8192
N_ROW = 8
N_COL = 2


def draw_tile_counts(key, part):
    first_key = jax.random.fold_in(key, 11)
    second_key = jax.random.fold_in(key, 23)
    counts_flat = jax.random.randint(first_key, (N_ROW * N_COL,), 1, TILES_DEV + 1)
    chosen = jax.random.randint(second_key, (), 0, N_ROW * N_COL)
    counts_flat = counts_flat.at[chosen].set(TILES_DEV)
    return counts_flat.reshape(N_ROW, N_COL).astype(jnp.int32)


def place_ends(array, key, smallest, top_value):
    longest = array.shape.index(max(array.shape))
    spots = []
    for shift in (0, 1):
        where = [jax.random.randint(jax.random.fold_in(key, axis), (), 0, length) for axis, length in enumerate(array.shape)]
        where[longest] = (where[longest] + shift) % array.shape[longest]
        spots.append(tuple(where))
    return array.at[spots[0]].set(smallest).at[spots[1]].set(top_value)


def block_scale(own_key, dims, shards, low, high):
    def one(dim, blocks):
        heights = jax.random.uniform(jax.random.fold_in(jax.random.fold_in(own_key, 6), dim), (blocks,), jnp.float32, low / len(shards), high / len(shards))
        return jnp.repeat(jnp.exp(heights), dims[dim] // blocks).reshape((-1,) + (1,) * (len(dims) - dim - 1))

    gain = one(*shards[0])
    for cut in shards[1:]:
        gain = gain * one(*cut)
    return gain


def noise(key, dims, deviation, reach, cuts=(), held_as=jnp.bfloat16):
    array = deviation * jax.random.normal(key, dims, jnp.float32)
    if cuts:
        array = array * block_scale(key, dims, cuts, -0.22, 0.18)
    return jnp.clip(array, -reach, reach).astype(held_as)


def setup_inputs(seed: int = 0) -> dict:
    arg_keys = jax.random.split(jax.random.key(seed), 9)
    return {
        "adj_tiles": noise(arg_keys[0], (N_ROW, N_COL, TILES_DEV, BLOCK, BLOCK), BLOCK ** -0.5, 0.25, ((0, 8), (1, 2)), jnp.float32),
        "tile_rows": place_ends(jax.random.randint(arg_keys[1], (N_ROW, N_COL, TILES_DEV), 0, N_COL), jax.random.fold_in(arg_keys[1], 1), 0, N_COL - 1).astype(jnp.int32),
        "tile_cols": place_ends(jax.random.randint(arg_keys[2], (N_ROW, N_COL, TILES_DEV), 0, N_ROW), jax.random.fold_in(arg_keys[2], 1), 0, N_ROW - 1).astype(jnp.int32),
        "tile_counts": draw_tile_counts(jax.random.fold_in(arg_keys[8], 71), 0),
        "features_t": noise(arg_keys[4], (F, NODES), 1.0, 6.0, ((0, 2), (1, 16)), jnp.float32),
        "weight": noise(arg_keys[5], (F, F), F ** -0.5, 0.5, ((0, 2),), jnp.float32),
        "bias_vec": noise(arg_keys[6], (F,), 0.5, 3.0, (), jnp.float32),
        "cotangent": noise(arg_keys[7], (NODES, F), 0.003, 0.02, ((0, 32),), jnp.float32),
    }


def reference(adj_tiles, tile_rows, tile_cols, tile_counts, features_t, weight, bias_vec, cotangent):
    row_groups, col_groups, slot_count = tile_rows.shape
    block_len = adj_tiles.shape[-1]
    width = features_t.shape[0]
    node_feats = features_t.T.reshape(-1, block_len, width)
    row_global = (jnp.arange(row_groups, dtype=jnp.int32)[:, None, None] * col_groups + tile_rows).reshape(-1).astype(jnp.int32)
    col_global = (tile_cols * col_groups + jnp.arange(col_groups, dtype=jnp.int32)[None, :, None]).reshape(-1).astype(jnp.int32)
    is_live = (jnp.arange(slot_count, dtype=jnp.int32)[None, None, :] < tile_counts[:, :, None]).reshape(-1)
    flat_tiles = adj_tiles.reshape(-1, block_len, block_len)

    def add_tile(running, item):
        slab_one, row_block, col_block, usable = item
        contrib = jnp.dot(slab_one, node_feats[col_block], precision=lax.Precision.HIGHEST, preferred_element_type=jnp.float32)
        contrib = jnp.where(usable, contrib, jnp.zeros_like(contrib))
        return running.at[row_block].add(contrib), None

    start_sum = jnp.zeros(node_feats.shape, jnp.float32)
    summed, _ = lax.scan(add_tile, start_sum, (flat_tiles, row_global, col_global, is_live))
    mixed = summed.reshape(-1, width)
    preact = jnp.dot(mixed, weight, precision=lax.Precision.HIGHEST, preferred_element_type=jnp.float32) + bias_vec
    squash = jax.nn.sigmoid(preact)
    output = preact * squash
    slope = cotangent * squash * (1.0 + preact * (1.0 - squash))
    grad_weight = jnp.dot(mixed.T, slope, precision=lax.Precision.HIGHEST, preferred_element_type=jnp.float32)
    grad_bias = jnp.sum(slope, axis=0)
    return output, grad_weight, grad_bias
```

```python
import functools

import jax
import jax.numpy as jnp
from jax import lax
from jax.experimental import pallas as pl
from jax.experimental.pallas import tpu as pltpu
from jax.sharding import PartitionSpec as P

F32 = jnp.float32
BF16 = jnp.bfloat16
SUBLANES = 8


def dot(a, b, dims, precision=None):
    return lax.dot_general(a, b, (dims, ((), ())), precision=precision, preferred_element_type=F32)


def split(x):
    high = x.astype(BF16)
    return high, (x - high.astype(F32)).astype(BF16)


def split_kernel(slabs, high, low, held, sems):
    count = slabs.shape[0]
    copies = [pltpu.make_async_copy(slabs.at[t], held.at[t], sems.at[t]) for t in range(count)]
    for copy in copies:
        copy.start()
    for t, copy in enumerate(copies):
        copy.wait()
        high[t], low[t] = split(held[t])


def split_slabs(slabs):
    count = slabs.shape[0]
    return pl.pallas_call(
        split_kernel,
        out_shape=(pltpu.VMEM(slabs.shape, BF16), pltpu.VMEM(slabs.shape, BF16)),
        in_specs=[pl.BlockSpec(memory_space=pl.ANY)],
        out_specs=[pl.BlockSpec(memory_space=pltpu.VMEM)] * 2,
        scratch_shapes=[pltpu.VMEM(slabs.shape, F32), pltpu.SemaphoreType.DMA((count,))],
        compiler_params=pltpu.CompilerParams(vmem_limit_bytes=32 * 2**20),
        cost_estimate=pl.CostEstimate(flops=4 * slabs.size, bytes_accessed=8 * slabs.size, transcendentals=0),
        name="split_slabs",
    )(slabs)


def mix_kernel(sizes, sources, rows, cols, counts, slab_high, slab_low, *refs):
    groups, halves = sizes
    pieces, outs, (picked, total) = refs[: len(sources)], refs[len(sources) : -2], refs[-2:]
    slots = slab_high.shape[0]
    half_width, block = pieces[0].shape
    live = counts[0, 0]
    row, col, rep = lax.axis_index("row"), lax.axis_index("col"), lax.axis_index("rep")

    total[...] = jnp.zeros_like(total)
    for piece, source in zip(pieces, sources):
        block_id = source(row)

        @pl.loop(0, slots)
        def _(t):
            @pl.when((t < live) & (cols[0, 0, t] == block_id))
            def _():
                high, low = split(piece[...])
                picked[t, :half_width] = high
                picked[t, half_width:] = low

    for t in range(slots):

        @pl.when(t < live)
        def _():
            by_high = dot(picked[t], slab_high[t], ((1,), (1,)))
            by_low = dot(picked[t, :half_width], slab_low[t], ((1,), (1,)))
            total[rows[0, 0, t]] += by_high[:half_width] + by_high[half_width:] + by_low

    part = block // halves
    for k, out in enumerate(outs):
        for h in range(halves):
            begin = pl.multiple_of(lax.rem(rep + h, halves) * part, part)
            out[h] = total[lax.rem(col + k, groups), :, pl.ds(begin, part)]


def mix(sizes, sources, rows, cols, counts, slab_high, slab_low, pieces):
    groups, halves = sizes
    slots = slab_high.shape[0]
    half_width, block = pieces[0].shape
    out = jax.ShapeDtypeStruct((halves, half_width, block // halves), F32)
    return pl.pallas_call(
        functools.partial(mix_kernel, sizes, sources),
        out_shape=[out] * groups,
        in_specs=[pl.BlockSpec(memory_space=pltpu.SMEM)] * 3
        + [pl.BlockSpec(memory_space=pltpu.VMEM)] * (2 + len(pieces)),
        out_specs=[pl.BlockSpec(memory_space=pltpu.VMEM)] * groups,
        scratch_shapes=[
            pltpu.VMEM((slots, 2 * half_width, block), BF16),
            pltpu.VMEM((groups, half_width, block), F32),
        ],
        compiler_params=pltpu.CompilerParams(vmem_limit_bytes=32 * 2**20),
        name="mix",
    )(rows, cols, counts, slab_high, slab_low, *pieces)


def node_kernel(parts, *refs):
    highest = lax.Precision.HIGHEST
    (own, got), refs = refs[:2], refs[2:]
    others, refs = refs[: parts - 1], refs[parts - 1 :]
    weights, refs = refs[:parts], refs[parts:]
    bias, cotangent, output, *grads = refs
    mixed = [own[...] + got[...]] + [other[...] for other in others]
    preact = bias[...] + sum(dot(m, w[...], ((0,), (0,)), highest) for m, w in zip(mixed, weights))
    squash = 1.0 / (1.0 + jnp.exp(-preact))
    output[...] = preact * squash
    slope = cotangent[...] * squash * (1.0 + preact * (1.0 - squash))
    half_width = own.shape[0]
    bias_term = jnp.sum(slope, axis=0, keepdims=True)
    for k, (m, grad) in enumerate(zip(mixed, grads)):
        grad[:half_width] = dot(m, slope, ((1,), (0,)), highest)
        grad[half_width:] = jnp.broadcast_to(bias_term, (SUBLANES, bias_term.shape[1]))


def node_step(own, got, others, weights, bias, cotangent):
    parts = len(weights)
    half_width = own.shape[0]
    width = cotangent.shape[1]
    grad = jax.ShapeDtypeStruct((half_width + SUBLANES, width), F32)
    return pl.pallas_call(
        functools.partial(node_kernel, parts),
        out_shape=[jax.ShapeDtypeStruct(cotangent.shape, F32)] + [grad] * parts,
        in_specs=[pl.BlockSpec(memory_space=pltpu.VMEM)] * (4 + 2 * parts - 1),
        out_specs=[pl.BlockSpec(memory_space=pltpu.VMEM)] * (1 + parts),
        compiler_params=pltpu.CompilerParams(vmem_limit_bytes=32 * 2**20),
        name="node_step",
    )(own, got, *others, *weights, bias.reshape(1, width), cotangent)


def shift(x, axis, size, k, inner=1):
    outer = size // inner
    return lax.ppermute(x, axis, [(i, (i // inner + k) % outer * inner + i % inner) for i in range(size)])


def swap(x, axis, size, bit):
    return lax.ppermute(x, axis, [(i, i ^ bit) for i in range(size)])


def sum_over(x, axis, size):
    if size & (size - 1):
        return lax.psum(x, axis)
    bit = 1
    while bit < size:
        x = x + swap(x, axis, size, bit)
        bit *= 2
    return x


def local(row_size, groups, halves, adj_tiles, tile_rows, tile_cols, tile_counts, features_t, weight, bias_vec, cotangent):
    inner = 2 if row_size % 2 == 0 else 1
    outer = row_size // inner

    weights = [weight] + [shift(weight, "rep", halves, -k) for k in range(1, halves)]

    pieces, sources = [], []
    for k in range(outer):
        piece = shift(features_t, "row", row_size, k, inner) if k else features_t
        for j in range(inner):
            pieces.append(swap(piece, "row", row_size, j) if j else piece)
            sources.append(
                lambda row, k=k, j=j: lax.rem(row // inner + outer - k, outer) * inner + lax.bitwise_xor(row % inner, j)
            )
    slab_high, slab_low = split_slabs(adj_tiles[0, 0])
    parts = mix((groups, halves), sources, tile_rows, tile_cols, tile_counts, slab_high, slab_low, pieces)

    own = parts[0]
    got = shift(parts[1], "col", groups, 1) if groups > 1 else jnp.zeros_like(own)
    for k in range(2, groups):
        got = got + shift(parts[k], "col", groups, k)
    others = [shift(own[k] + got[k], "rep", halves, k) for k in range(1, halves)]
    output, *grads = node_step(own[0], got[0], others, _by_source(weights, halves), bias_vec, cotangent)
    grad = grads[0]
    for k in range(1, halves):
        grad = grad + shift(grads[k], "rep", halves, -k)
    grad = sum_over(grad, "col", groups)
    grad = sum_over(grad, "row", row_size)
    half_width = features_t.shape[0]
    return output, grad[:half_width], grad[half_width]


def _by_source(weights, halves):
    return [weights[0]] + [weights[halves - k] for k in range(1, halves)]


def solution(mesh):
    row_size, groups, halves = (mesh.shape[axis] for axis in ("row", "col", "rep"))
    in_specs = (
        P("row", "col", None, None, None),
        P("row", "col", None),
        P("row", "col", None),
        P("row", "col"),
        P("rep", ("row", "col")),
        P("rep", None),
        P(),
        P(("row", "col", "rep"), None),
    )
    out_specs = (P(("row", "col", "rep"), None), P("rep", None), P())
    return jax.shard_map(
        functools.partial(local, row_size, groups, halves),
        mesh=mesh,
        in_specs=in_specs,
        out_specs=out_specs,
        check_vma=False,
    )
```

```python
import functools

import jax
import jax.numpy as jnp
from jax import lax
from jax.experimental import pallas as pl
from jax.experimental.pallas import tpu as pltpu
from jax.sharding import PartitionSpec as P

F32 = jnp.float32
BF16 = jnp.bfloat16
SUBLANES = 8
VMEM_BYTES = 40 * 2**20


def dot(a, b, dims=((1,), (0,))):
    return lax.dot_general(a, b, (dims, ((), ())), preferred_element_type=F32)


def split(x):
    high = x.astype(BF16)
    return high, (x - high.astype(F32)).astype(BF16)


def dot_split(a, b, dims):
    (ah, al), (bh, bl) = a, b
    return dot(ah, bh, dims) + (dot(ah, bl, dims) + dot(al, bh, dims))


def call(kernel, out_shape, spaces, name, scratch=(), cost=None):
    return pl.pallas_call(
        kernel,
        out_shape=out_shape,
        in_specs=[pl.BlockSpec(memory_space=space) for space in spaces],
        out_specs=jax.tree.map(lambda _: pl.BlockSpec(memory_space=pltpu.VMEM), out_shape),
        scratch_shapes=list(scratch),
        compiler_params=pltpu.CompilerParams(vmem_limit_bytes=VMEM_BYTES),
        cost_estimate=cost,
        name=name,
    )


def split_kernel(slabs, high, low, held, sems):
    count = slabs.shape[0]
    copies = [pltpu.make_async_copy(slabs.at[t], held.at[t], sems.at[t]) for t in range(count)]
    for copy in copies:
        copy.start()
    for t, copy in enumerate(copies):
        copy.wait()
        high[t], low[t] = split(held[t].T)


def split_slabs(slabs):
    count = slabs.shape[0]
    out = pltpu.VMEM(slabs.shape, BF16)
    scratch = [pltpu.VMEM(slabs.shape, F32), pltpu.SemaphoreType.DMA((count,))]
    cost = pl.CostEstimate(flops=4 * slabs.size, bytes_accessed=8 * slabs.size, transcendentals=0)
    return call(split_kernel, (out, out), [pl.ANY], "split_slabs", scratch, cost)(
        pltpu.with_memory_space_constraint(slabs, pltpu.HBM)
    )


def product(piece, high, low):
    half_width = piece.shape[0] // 2
    by_high = dot(piece, high)
    return by_high[:half_width] + by_high[half_width:] + dot(piece[:half_width], low)


def pick(picked, t, piece):
    half_width = piece.shape[0]
    picked[t, :half_width], picked[t, half_width:] = split(piece[...])


def early_kernel(sources, rows, cols, counts, high, low, *refs):
    pieces, (total, picked, found) = refs[: len(sources)], refs[-3:]
    slots = high.shape[0]
    live = counts[0, 0]
    row = lax.axis_index("row")
    for t in range(slots):
        found[t] = 0
    for piece, source in zip(pieces, sources):
        block = source(row)

        @pl.loop(0, slots)
        def _(t):
            @pl.when((t < live) & (cols[0, 0, t] == block))
            def _():
                found[t] = 1
                pick(picked, t, piece)

    total[...] = jnp.zeros_like(total)
    for t in range(slots):

        @pl.when(found[t] == 1)
        def _():
            total[rows[0, 0, t]] += product(picked[t], high[t], low[t])


def late_kernel(sizes, sources, rows, cols, counts, high, low, early, *refs):
    groups, halves = sizes
    pieces, outs, (total, picked) = refs[: len(sources)], refs[len(sources) : -2], refs[-2:]
    slots = high.shape[0]
    block_len = early.shape[2]
    live = counts[0, 0]
    row, col, rep = lax.axis_index("row"), lax.axis_index("col"), lax.axis_index("rep")
    total[...] = early[...]
    for piece, source in zip(pieces, sources):
        block = source(row)
        pick(picked, 0, piece)
        for t in range(slots):

            @pl.when((t < live) & (cols[0, 0, t] == block))
            def _():
                total[rows[0, 0, t]] += product(picked[0], high[t], low[t])

    part = block_len // halves
    for k, out in enumerate(outs):
        for h in range(halves):
            begin = pl.multiple_of(lax.rem(rep + h, halves) * part, part)
            out[h] = total[lax.rem(col + k, groups), :, pl.ds(begin, part)]


def mix(sizes, slot_info, slabs, early, late):
    groups, halves = sizes
    slots = slabs[0].shape[0]
    half_width, block_len = early[0][0].shape
    spaces = [pltpu.SMEM] * 3 + [pltpu.VMEM] * 2
    picked = pltpu.VMEM((slots, 2 * half_width, block_len), BF16)
    pieces, sources = zip(*early)
    total = call(
        functools.partial(early_kernel, sources),
        pltpu.VMEM((groups, half_width, block_len), F32),
        spaces + [pltpu.VMEM] * len(pieces),
        "mix_early",
        [picked, pltpu.SMEM((slots,), jnp.int32)],
        pl.CostEstimate(flops=6 * slabs[0].size * half_width, bytes_accessed=4 * slabs[0].size, transcendentals=0),
    )(*slot_info, *slabs, *pieces)
    pieces, sources = zip(*late)
    return call(
        functools.partial(late_kernel, sizes, sources),
        [pltpu.VMEM((halves, half_width, block_len // halves), F32)] * groups,
        spaces + [pltpu.VMEM] * (1 + len(pieces)),
        "mix_late",
        [pltpu.VMEM(total.shape, F32), picked],
    )(*slot_info, *slabs, total, *pieces)


def node_kernel(parts, *refs):
    (own, got), refs = refs[:2], refs[2:]
    others, refs = refs[: parts - 1], refs[parts - 1 :]
    weights, refs = refs[:parts], refs[parts:]
    bias, cotangent, output, *grads = refs
    half_width = own.shape[0]
    mixed = split(jnp.concatenate([own[...] + got[...]] + [other[...] for other in others]))
    weight = split(jnp.concatenate([w[...] for w in weights]))
    preact = bias[...] + dot_split(mixed, weight, ((0,), (0,)))
    squash = 1.0 / (1.0 + jnp.exp(-preact))
    output[...] = preact * squash
    slope = cotangent[...] * squash * (1.0 + preact * (1.0 - squash))
    bias_term = jnp.sum(slope, axis=0, keepdims=True)
    product = dot_split(mixed, split(slope), ((1,), (0,)))
    for k, grad in enumerate(grads):
        grad[:half_width] = product[k * half_width : (k + 1) * half_width]
        grad[half_width:] = jnp.broadcast_to(bias_term, (SUBLANES, bias_term.shape[1]))


def node_step(own, got, others, weights, bias, cotangent):
    parts = len(weights)
    width = cotangent.shape[1]
    grad = pltpu.VMEM((own.shape[0] + SUBLANES, width), F32)
    return call(
        functools.partial(node_kernel, parts),
        [pltpu.VMEM(cotangent.shape, F32)] + [grad] * parts,
        [pltpu.VMEM] * (4 + 2 * parts - 1),
        "node_step",
    )(own, got, *others, *weights, bias.reshape(1, width), cotangent)


def last_kernel(a, b, grad_weight, grad_bias):
    half_width = grad_weight.shape[0]
    grad_weight[...] = a[:half_width] + b[:half_width]
    grad_bias[...] = a[half_width] + b[half_width]


def last_step(a, b):
    half_width, width = a.shape[0] - SUBLANES, a.shape[1]
    out = [jax.ShapeDtypeStruct((half_width, width), F32), jax.ShapeDtypeStruct((width,), F32)]
    return call(last_kernel, out, [pltpu.VMEM] * 2, "last_step")(a, b)


def shift(x, axis, size, k):
    return lax.ppermute(x, axis, [(i, (i + k) % size) for i in range(size)])


def swap(x, axis, size, bit):
    return lax.ppermute(x, axis, [(i, i ^ bit) for i in range(size)])


def swap_two(x, axes, sizes, bits):
    (_, minor), perm = sizes, []
    for i in range(sizes[0]):
        for j in range(minor):
            perm.append((i * minor + j, (i ^ bits[0]) * minor + (j ^ bits[1])))
    return lax.ppermute(x, axes, perm)


def is_power(n):
    return n & (n - 1) == 0


def gather_row(x, size, held):
    if not is_power(size) or size < 2:
        pieces = [x] + [shift(x, "row", size, k) for k in range(1, size)]
        return [(p, lambda row, k=k: lax.rem(row + size - k, size)) for k, p in enumerate(pieces)], held
    found = {0: x}
    bit = size // 2
    while bit > 1:
        for mask in list(found):
            found[mask ^ bit] = swap(found[mask], "row", size, bit)
        if bit == size // 2:
            found[bit], held = lax.optimization_barrier((found[bit], held))
        bit //= 2
    order = sorted(found, key=lambda mask: (bin(mask).count("1"), mask))
    crossed = {0: swap(x, "row", size, 1)}
    first, _ = lax.optimization_barrier((found[order[1]], crossed[0])) if len(order) > 1 else (x, x)
    for mask in order[1:]:
        crossed[mask] = swap(first if mask == order[1] else found[mask], "row", size, 1)
    far = [(mask ^ 1, crossed[mask]) for mask in order]
    near = [(mask, found[mask]) for mask in order]
    return [(p, lambda row, mask=mask: lax.bitwise_xor(row, mask)) for mask, p in near + far], held


def sum_all(grad, groups, row_size):
    if not (is_power(groups) and is_power(row_size)) or groups * row_size == 1:
        grad = lax.psum(grad, ("row", "col"))
        return grad, jnp.zeros_like(grad)
    col_bits = [1 << i for i in range(groups.bit_length() - 1)]
    row_bits = [1 << i for i in range(row_size.bit_length() - 1)]
    steps = []
    if col_bits and row_bits:
        axes, sizes, a, b = ("row", "col"), (row_size, groups), row_bits.pop(0), col_bits.pop(0)

        def square(x):
            one = swap_two(x, axes, sizes, (a, 0))
            two = swap_two(x, axes, sizes, (0, b))
            both = swap_two(x, axes, sizes, (a, b))
            return x + one, two + both

        steps.append(square)
    steps += [lambda x, bit=bit: (x, swap(x, "col", groups, bit)) for bit in col_bits]
    steps += [lambda x, bit=bit: (x, swap(x, "row", row_size, bit)) for bit in row_bits]
    for step in steps[:-1]:
        a, b = step(grad)
        grad = a + b
    return steps[-1](grad)


def local(row_size, groups, halves, adj_tiles, tile_rows, tile_cols, tile_counts, features_t, weight, bias_vec, cotangent):
    weights = [weight] + [shift(weight, "rep", halves, k) for k in range(1, halves)]
    pieces, (slabs, weights) = gather_row(features_t, row_size, (split_slabs(adj_tiles[0, 0]), weights))
    slot_info = (tile_rows, tile_cols, tile_counts)
    parts = mix((groups, halves), slot_info, slabs, pieces[:-1], pieces[-1:])

    own = parts[0]
    got = shift(parts[1], "col", groups, 1) if groups > 1 else jnp.zeros_like(own)
    for k in range(2, groups):
        got = got + shift(parts[k], "col", groups, k)
    others = [shift(own[k] + got[k], "rep", halves, k) for k in range(1, halves)]
    output, *grads = node_step(own[0], got[0], others, weights, bias_vec, cotangent)
    grad = grads[0]
    for k in range(1, halves):
        grad = grad + shift(grads[k], "rep", halves, -k)
    grad_weight, grad_bias = last_step(*sum_all(grad, groups, row_size))
    return output, grad_weight, grad_bias


def solution(mesh):
    row_size, groups, halves = (mesh.shape[axis] for axis in ("row", "col", "rep"))
    in_specs = (
        P("row", "col", None, None, None),
        P("row", "col", None),
        P("row", "col", None),
        P("row", "col"),
        P("rep", ("row", "col")),
        P("rep", None),
        P(),
        P(("row", "col", "rep"), None),
    )
    out_specs = (P(("row", "col", "rep"), None), P("rep", None), P())
    return jax.shard_map(
        functools.partial(local, row_size, groups, halves),
        mesh=mesh,
        in_specs=in_specs,
        out_specs=out_specs,
        check_vma=False,
    )
```

```python
import functools

import jax
import jax.numpy as jnp
from jax import lax
from jax.experimental import pallas as pl
from jax.experimental.pallas import tpu as pltpu
from jax.sharding import PartitionSpec as P

F32 = jnp.float32
BF16 = jnp.bfloat16
SUBLANES = 8
VMEM_BYTES = 40 * 2**20


def dot(a, b, dims=((1,), (0,))):
    return lax.dot_general(a, b, (dims, ((), ())), preferred_element_type=F32)


def split(x):
    high = x.astype(BF16)
    return high, (x - high.astype(F32)).astype(BF16)


def dot_split(a, b, dims):
    (ah, al), (bh, bl) = a, b
    return dot(ah, bh, dims) + (dot(ah, bl, dims) + dot(al, bh, dims))


def call(kernel, out_shape, spaces, name, scratch=(), cost=None):
    return pl.pallas_call(
        kernel,
        out_shape=out_shape,
        in_specs=[pl.BlockSpec(memory_space=space) for space in spaces],
        out_specs=jax.tree.map(lambda _: pl.BlockSpec(memory_space=pltpu.VMEM), out_shape),
        scratch_shapes=list(scratch),
        compiler_params=pltpu.CompilerParams(vmem_limit_bytes=VMEM_BYTES),
        cost_estimate=cost,
        name=name,
    )


def split_kernel(slabs, high, low, held, sems):
    count = slabs.shape[0]
    copies = [pltpu.make_async_copy(slabs.at[t], held.at[t], sems.at[t]) for t in range(count)]
    for copy in copies:
        copy.start()
    for t, copy in enumerate(copies):
        copy.wait()
        high[t], low[t] = split(held[t].T)


def split_slabs(slabs):
    count = slabs.shape[0]
    out = pltpu.VMEM(slabs.shape, BF16)
    scratch = [pltpu.VMEM(slabs.shape, F32), pltpu.SemaphoreType.DMA((count,))]
    cost = pl.CostEstimate(flops=4 * slabs.size, bytes_accessed=8 * slabs.size, transcendentals=0)
    return call(split_kernel, (out, out), [pl.ANY], "split_slabs", scratch, cost)(
        pltpu.with_memory_space_constraint(slabs, pltpu.HBM)
    )


def product(piece, high, low):
    half_width = piece.shape[0] // 2
    by_high = dot(piece, high)
    return by_high[:half_width] + by_high[half_width:] + dot(piece[:half_width], low)


def pick(picked, t, piece):
    half_width = piece.shape[0]
    picked[t, :half_width], picked[t, half_width:] = split(piece[...])


def early_kernel(sources, rows, cols, counts, high, low, *refs):
    pieces, (total, picked, found) = refs[: len(sources)], refs[-3:]
    slots = high.shape[0]
    live = counts[0, 0]
    row = lax.axis_index("row")
    for t in range(slots):
        found[t] = 0
    for piece, source in zip(pieces, sources):
        block = source(row)

        @pl.loop(0, slots)
        def _(t):
            @pl.when((t < live) & (cols[0, 0, t] == block))
            def _():
                found[t] = 1
                pick(picked, t, piece)

    total[...] = jnp.zeros_like(total)
    for t in range(slots):

        @pl.when(found[t] == 1)
        def _():
            total[rows[0, 0, t]] += product(picked[t], high[t], low[t])


def late_kernel(sizes, sources, rows, cols, counts, high, low, early, *refs):
    groups, halves = sizes
    pieces, outs, (total, picked) = refs[: len(sources)], refs[len(sources) : -2], refs[-2:]
    slots = high.shape[0]
    block_len = early.shape[2]
    live = counts[0, 0]
    row, col, rep = lax.axis_index("row"), lax.axis_index("col"), lax.axis_index("rep")
    total[...] = early[...]
    for piece, source in zip(pieces, sources):
        block = source(row)
        pick(picked, 0, piece)
        for t in range(slots):

            @pl.when((t < live) & (cols[0, 0, t] == block))
            def _():
                total[rows[0, 0, t]] += product(picked[0], high[t], low[t])

    part = block_len // halves
    for i, out in enumerate(outs):
        k, h = divmod(i, halves)
        begin = pl.multiple_of(lax.rem(rep + h, halves) * part, part)
        out[...] = total[lax.rem(col + k, groups), :, pl.ds(begin, part)]


def mix(sizes, slot_info, slabs, early, late):
    groups, halves = sizes
    slots = slabs[0].shape[0]
    half_width, block_len = early[0][0].shape
    spaces = [pltpu.SMEM] * 3 + [pltpu.VMEM] * 2
    picked = pltpu.VMEM((slots, 2 * half_width, block_len), BF16)
    pieces, sources = zip(*early)
    total = call(
        functools.partial(early_kernel, sources),
        pltpu.VMEM((groups, half_width, block_len), F32),
        spaces + [pltpu.VMEM] * len(pieces),
        "mix_early",
        [picked, pltpu.SMEM((slots,), jnp.int32)],
        pl.CostEstimate(flops=6 * slabs[0].size * half_width, bytes_accessed=4 * slabs[0].size, transcendentals=0),
    )(*slot_info, *slabs, *pieces)
    pieces, sources = zip(*late)
    return call(
        functools.partial(late_kernel, sizes, sources),
        [pltpu.VMEM((half_width, block_len // halves), F32)] * (groups * halves),
        spaces + [pltpu.VMEM] * (1 + len(pieces)),
        "mix_late",
        [pltpu.VMEM(total.shape, F32), picked],
    )(*slot_info, *slabs, total, *pieces)


def node_kernel(groups, halves, *refs):
    terms, refs = refs[: groups * halves], refs[groups * halves :]
    weights, (bias, cotangent, output, *grads) = refs[:halves], refs[halves:]
    half_width = terms[0].shape[0]
    mixed = [sum(terms[k * halves + h][...] for k in range(groups)) for h in range(halves)]
    mixed = split(jnp.concatenate(mixed))
    weight = split(jnp.concatenate([w[...] for w in weights]))
    preact = bias[...] + dot_split(mixed, weight, ((0,), (0,)))
    squash = 1.0 / (1.0 + jnp.exp(-preact))
    output[...] = preact * squash
    slope = cotangent[...] * squash * (1.0 + preact * (1.0 - squash))
    bias_term = jnp.sum(slope, axis=0, keepdims=True)
    product = dot_split(mixed, split(slope), ((1,), (0,)))
    for h, grad in enumerate(grads):
        grad[:half_width] = product[h * half_width : (h + 1) * half_width]
        grad[half_width:] = jnp.broadcast_to(bias_term, (SUBLANES, bias_term.shape[1]))


def node_step(sizes, terms, weights, bias, cotangent):
    groups, halves = sizes
    width = cotangent.shape[1]
    grad = pltpu.VMEM((terms[0].shape[0] + SUBLANES, width), F32)
    return call(
        functools.partial(node_kernel, groups, halves),
        [pltpu.VMEM(cotangent.shape, F32)] + [grad] * halves,
        [pltpu.VMEM] * (len(terms) + halves + 2),
        "node_step",
    )(*terms, *weights, bias.reshape(1, width), cotangent)


def last_kernel(a, b, grad_weight, grad_bias):
    half_width = grad_weight.shape[0]
    grad_weight[...] = a[:half_width] + b[:half_width]
    grad_bias[...] = a[half_width] + b[half_width]


def last_step(a, b):
    half_width, width = a.shape[0] - SUBLANES, a.shape[1]
    out = [jax.ShapeDtypeStruct((half_width, width), F32), jax.ShapeDtypeStruct((width,), F32)]
    return call(last_kernel, out, [pltpu.VMEM] * 2, "last_step")(a, b)


def shift(x, axis, size, k):
    return lax.ppermute(x, axis, [(i, (i + k) % size) for i in range(size)])


def shift_two(x, sizes, steps):
    (groups, halves), (k, h) = sizes, steps
    perm = [
        (c * halves + r, (c + k) % groups * halves + (r + h) % halves) for c in range(groups) for r in range(halves)
    ]
    return lax.ppermute(x, ("col", "rep"), perm)


def swap(x, axis, size, bit):
    return lax.ppermute(x, axis, [(i, i ^ bit) for i in range(size)])


def swap_two(x, axes, sizes, bits):
    (_, minor), perm = sizes, []
    for i in range(sizes[0]):
        for j in range(minor):
            perm.append((i * minor + j, (i ^ bits[0]) * minor + (j ^ bits[1])))
    return lax.ppermute(x, axes, perm)


def is_power(n):
    return n & (n - 1) == 0


def gather_row(x, size, held):
    if not is_power(size) or size < 2:
        pieces = [x] + [shift(x, "row", size, k) for k in range(1, size)]
        return [(p, lambda row, k=k: lax.rem(row + size - k, size)) for k, p in enumerate(pieces)], held
    found = {0: x}
    own_cross = swap(x, "row", size, 1)
    bit = size // 2
    while bit > 1:
        for mask in list(found):
            found[mask ^ bit] = swap(found[mask], "row", size, bit)
        if bit == size // 2:
            found[bit], own_cross, held = lax.optimization_barrier((found[bit], own_cross, held))
        bit //= 2
    order = sorted(found, key=lambda mask: (bin(mask).count("1"), mask))
    crossed = {0: own_cross}
    for mask in order[1:]:
        direct = is_power(mask) and mask < size // 2
        crossed[mask] = swap(x, "row", size, mask ^ 1) if direct else None
    for mask in order[1:]:
        if crossed[mask] is None:
            passed = found[mask]
            if mask == order[-1] and size > 4:
                passed, _ = lax.optimization_barrier((passed, crossed[order[1]]))
            crossed[mask] = swap(passed, "row", size, 1)
    far = [(mask ^ 1, crossed[mask]) for mask in order]
    near = [(mask, found[mask]) for mask in order]
    return [(p, lambda row, mask=mask: lax.bitwise_xor(row, mask)) for mask, p in near + far], held


def sum_all(grad, groups, row_size):
    if not (is_power(groups) and is_power(row_size)) or groups * row_size == 1:
        grad = lax.psum(grad, ("row", "col"))
        return grad, jnp.zeros_like(grad)
    col_bits = [1 << i for i in range(groups.bit_length() - 1)]
    row_bits = [1 << i for i in range(row_size.bit_length() - 1)]
    steps = []
    if col_bits and row_bits:
        axes, sizes, a, b = ("row", "col"), (row_size, groups), row_bits.pop(0), col_bits.pop(0)

        def square(x):
            one = swap_two(x, axes, sizes, (a, 0))
            two = swap_two(x, axes, sizes, (0, b))
            both = swap_two(x, axes, sizes, (a, b))
            return x + one, two + both

        steps.append(square)
    steps += [lambda x, bit=bit: (x, swap(x, "col", groups, bit)) for bit in col_bits]
    while row_bits:
        (one, two), row_bits = (row_bits + [0])[:2], row_bits[2:]
        if two:
            steps.append(
                lambda x, one=one, two=two: (
                    x + swap(x, "row", row_size, one),
                    swap(x, "row", row_size, two) + swap(x, "row", row_size, one ^ two),
                )
            )
        else:
            steps.append(lambda x, one=one: (x, swap(x, "row", row_size, one)))
    for step in steps[:-1]:
        a, b = step(grad)
        grad = a + b
    return steps[-1](grad)


def local(row_size, groups, halves, adj_tiles, tile_rows, tile_cols, tile_counts, features_t, weight, bias_vec, cotangent):
    weights = [weight] + [shift(weight, "rep", halves, k) for k in range(1, halves)]
    pieces, (slabs, weights) = gather_row(features_t, row_size, (split_slabs(adj_tiles[0, 0]), weights))
    slot_info = (tile_rows, tile_cols, tile_counts)
    parts = mix((groups, halves), slot_info, slabs, pieces[:-1], pieces[-1:])

    terms = [shift_two(part, (groups, halves), divmod(i, halves)) if i else part for i, part in enumerate(parts)]
    output, *grads = node_step((groups, halves), terms, weights, bias_vec, cotangent)
    grad = grads[0]
    for k in range(1, halves):
        grad = grad + shift(grads[k], "rep", halves, -k)
    grad_weight, grad_bias = last_step(*sum_all(grad, groups, row_size))
    return output, grad_weight, grad_bias


def solution(mesh):
    row_size, groups, halves = (mesh.shape[axis] for axis in ("row", "col", "rep"))
    in_specs = (
        P("row", "col", None, None, None),
        P("row", "col", None),
        P("row", "col", None),
        P("row", "col"),
        P("rep", ("row", "col")),
        P("rep", None),
        P(),
        P(("row", "col", "rep"), None),
    )
    out_specs = (P(("row", "col", "rep"), None), P("rep", None), P())
    return jax.shard_map(
        functools.partial(local, row_size, groups, halves),
        mesh=mesh,
        in_specs=in_specs,
        out_specs=out_specs,
        check_vma=False,
    )
```

```python
import functools

import jax
import jax.numpy as jnp
from jax import lax
from jax.experimental import pallas as pl
from jax.experimental.pallas import tpu as pltpu
from jax.sharding import PartitionSpec as P

F32 = jnp.float32
BF16 = jnp.bfloat16
SUBLANES = 8
VMEM_BYTES = 40 * 2**20


def dot(a, b, dims=((1,), (0,))):
    return lax.dot_general(a, b, (dims, ((), ())), preferred_element_type=F32)


def split(x):
    high = x.astype(BF16)
    return high, (x - high.astype(F32)).astype(BF16)


def dot_split(a, b, dims):
    (ah, al), (bh, bl) = a, b
    return dot(ah, bh, dims) + (dot(ah, bl, dims) + dot(al, bh, dims))


def call(kernel, out_shape, spaces, name, scratch=(), cost=None):
    return pl.pallas_call(
        kernel,
        out_shape=out_shape,
        in_specs=[pl.BlockSpec(memory_space=space) for space in spaces],
        out_specs=jax.tree.map(lambda _: pl.BlockSpec(memory_space=pltpu.VMEM), out_shape),
        scratch_shapes=list(scratch),
        compiler_params=pltpu.CompilerParams(vmem_limit_bytes=VMEM_BYTES),
        cost_estimate=cost,
        name=name,
    )


def split_kernel(slabs, high, low, held, sems):
    count = slabs.shape[0]
    copies = [pltpu.make_async_copy(slabs.at[t], held.at[t], sems.at[t]) for t in range(count)]
    for copy in copies:
        copy.start()
    for t, copy in enumerate(copies):
        copy.wait()
        high[t], low[t] = split(held[t].T)


def split_slabs(slabs):
    count = slabs.shape[0]
    out = pltpu.VMEM(slabs.shape, BF16)
    scratch = [pltpu.VMEM(slabs.shape, F32), pltpu.SemaphoreType.DMA((count,))]
    cost = pl.CostEstimate(flops=4 * slabs.size, bytes_accessed=8 * slabs.size, transcendentals=0)
    return call(split_kernel, (out, out), [pl.ANY], "split_slabs", scratch, cost)(
        pltpu.with_memory_space_constraint(slabs, pltpu.HBM)
    )


def product(piece, high, low):
    half_width = piece.shape[0] // 2
    by_high = dot(piece, high)
    return by_high[:half_width] + by_high[half_width:] + dot(piece[:half_width], low)


def pick(picked, t, piece):
    half_width = piece.shape[0]
    picked[t, :half_width], picked[t, half_width:] = split(piece[...])


def early_kernel(sources, rows, cols, counts, high, low, *refs):
    pieces, (total, picked, found) = refs[: len(sources)], refs[-3:]
    slots = high.shape[0]
    live = counts[0, 0]
    row = lax.axis_index("row")
    for t in range(slots):
        found[t] = 0
    for piece, source in zip(pieces, sources):
        block = source(row)

        @pl.loop(0, slots)
        def _(t):
            @pl.when((t < live) & (cols[0, 0, t] == block))
            def _():
                found[t] = 1
                pick(picked, t, piece)

    total[...] = jnp.zeros_like(total)
    for t in range(slots):

        @pl.when(found[t] == 1)
        def _():
            total[rows[0, 0, t]] += product(picked[t], high[t], low[t])


def late_kernel(sizes, sources, rows, cols, counts, high, low, early, *refs):
    groups, halves = sizes
    pieces, outs, (total, picked) = refs[: len(sources)], refs[len(sources) : -2], refs[-2:]
    slots = high.shape[0]
    block_len = early.shape[2]
    live = counts[0, 0]
    row, col, rep = lax.axis_index("row"), lax.axis_index("col"), lax.axis_index("rep")
    total[...] = early[...]
    for piece, source in zip(pieces, sources):
        block = source(row)
        pick(picked, 0, piece)
        for t in range(slots):

            @pl.when((t < live) & (cols[0, 0, t] == block))
            def _():
                total[rows[0, 0, t]] += product(picked[0], high[t], low[t])

    part = block_len // halves
    for i, out in enumerate(outs):
        k, h = divmod(i, halves)
        begin = pl.multiple_of(lax.rem(rep + h, halves) * part, part)
        out[...] = total[lax.rem(col + k, groups), :, pl.ds(begin, part)]


def mix(sizes, slot_info, slabs, early, late):
    groups, halves = sizes
    slots = slabs[0].shape[0]
    half_width, block_len = early[0][0].shape
    spaces = [pltpu.SMEM] * 3 + [pltpu.VMEM] * 2
    picked = pltpu.VMEM((slots, 2 * half_width, block_len), BF16)
    pieces, sources = zip(*early)
    total = call(
        functools.partial(early_kernel, sources),
        pltpu.VMEM((groups, half_width, block_len), F32),
        spaces + [pltpu.VMEM] * len(pieces),
        "mix_early",
        [picked, pltpu.SMEM((slots,), jnp.int32)],
        pl.CostEstimate(flops=6 * slabs[0].size * half_width, bytes_accessed=4 * slabs[0].size, transcendentals=0),
    )(*slot_info, *slabs, *pieces)
    pieces, sources = zip(*late)
    return call(
        functools.partial(late_kernel, sizes, sources),
        [pltpu.VMEM((half_width, block_len // halves), F32)] * (groups * halves),
        spaces + [pltpu.VMEM] * (1 + len(pieces)),
        "mix_late",
        [pltpu.VMEM(total.shape, F32), picked],
    )(*slot_info, *slabs, total, *pieces)


def node_kernel(groups, halves, *refs):
    terms, refs = refs[: groups * halves], refs[groups * halves :]
    weights, (bias, cotangent, output, *grads) = refs[:halves], refs[halves:]
    half_width = terms[0].shape[0]
    mixed = [sum(terms[k * halves + h][...] for k in range(groups)) for h in range(halves)]
    mixed = split(jnp.concatenate(mixed))
    weight = split(jnp.concatenate([w[...] for w in weights]))
    preact = bias[...] + dot_split(mixed, weight, ((0,), (0,)))
    squash = 1.0 / (1.0 + jnp.exp(-preact))
    output[...] = preact * squash
    slope = cotangent[...] * squash * (1.0 + preact * (1.0 - squash))
    bias_term = jnp.sum(slope, axis=0, keepdims=True)
    product = dot_split(mixed, split(slope), ((1,), (0,)))
    for h, grad in enumerate(grads):
        grad[:half_width] = product[h * half_width : (h + 1) * half_width]
        grad[half_width:] = jnp.broadcast_to(bias_term, (SUBLANES, bias_term.shape[1]))


def node_step(sizes, terms, weights, bias, cotangent):
    groups, halves = sizes
    width = cotangent.shape[1]
    grad = pltpu.VMEM((terms[0].shape[0] + SUBLANES, width), F32)
    return call(
        functools.partial(node_kernel, groups, halves),
        [pltpu.VMEM(cotangent.shape, F32)] + [grad] * halves,
        [pltpu.VMEM] * (len(terms) + halves + 2),
        "node_step",
    )(*terms, *weights, bias.reshape(1, width), cotangent)


def last_kernel(a, b, grad_weight, grad_bias):
    half_width = grad_weight.shape[0]
    grad_weight[...] = a[:half_width] + b[:half_width]
    grad_bias[...] = a[half_width] + b[half_width]


def last_step(a, b):
    half_width, width = a.shape[0] - SUBLANES, a.shape[1]
    out = [jax.ShapeDtypeStruct((half_width, width), F32), jax.ShapeDtypeStruct((width,), F32)]
    return call(last_kernel, out, [pltpu.VMEM] * 2, "last_step")(a, b)


def shift(x, axis, size, k):
    return lax.ppermute(x, axis, [(i, (i + k) % size) for i in range(size)])


def shift_two(x, sizes, steps):
    (groups, halves), (k, h) = sizes, steps
    perm = [
        (c * halves + r, (c + k) % groups * halves + (r + h) % halves) for c in range(groups) for r in range(halves)
    ]
    return lax.ppermute(x, ("col", "rep"), perm)


def swap(x, axis, size, bit):
    return lax.ppermute(x, axis, [(i, i ^ bit) for i in range(size)])


def swap_two(x, axes, sizes, bits):
    (_, minor), perm = sizes, []
    for i in range(sizes[0]):
        for j in range(minor):
            perm.append((i * minor + j, (i ^ bits[0]) * minor + (j ^ bits[1])))
    return lax.ppermute(x, axes, perm)


def is_power(n):
    return n & (n - 1) == 0


def gather_row(x, size, held):
    if not is_power(size) or size < 2:
        pieces = [x] + [shift(x, "row", size, k) for k in range(1, size)]
        return [(p, lambda row, k=k: lax.rem(row + size - k, size)) for k, p in enumerate(pieces)], held
    bits = [1 << i for i in range(1, size.bit_length() - 1)]
    basis = [size - 2] + bits[-2::-1] if bits else []
    own_cross = swap(x, "row", size, 1)
    found = {0: x}
    for step, mask in enumerate(basis):
        new = {}
        for other, block in found.items():
            new[other ^ mask] = swap(block, "row", size, mask)
        if step == 0:
            near = swap(x, "row", size, basis[-1]) if len(basis) > 1 else x
            new[mask], own_cross, held = lax.optimization_barrier((new[mask], own_cross, held))
        elif step == len(basis) - 1:
            new[mask] = near
        found.update(new)
    crossed = {0: own_cross}
    if len(basis) > 1:
        crossed[basis[-1]] = swap(x, "row", size, basis[-1] ^ 1)
    last = None
    for mask, block in found.items():
        if mask not in crossed:
            if mask not in basis and last is None:
                last = mask
                block, _ = lax.optimization_barrier((block, crossed[basis[-1]]))
            crossed[mask] = swap(block, "row", size, 1)
    order = sorted(found, key=lambda mask: (mask == last, mask not in basis and mask != 0, mask))
    far = [(mask ^ 1, crossed[mask]) for mask in order]
    near = [(mask, found[mask]) for mask in order]
    return [(p, lambda row, mask=mask: lax.bitwise_xor(row, mask)) for mask, p in near + far], held


def sum_all(grad, groups, row_size):
    if not (is_power(groups) and is_power(row_size)) or groups * row_size == 1:
        grad = lax.psum(grad, ("row", "col"))
        return grad, jnp.zeros_like(grad)
    col_bits = [1 << i for i in range(groups.bit_length() - 1)]
    row_bits = [1 << i for i in range(row_size.bit_length() - 1)]
    steps = []
    if col_bits and row_bits:
        axes, sizes, a, b = ("row", "col"), (row_size, groups), row_bits.pop(0), col_bits.pop(0)

        def square(x):
            one = swap_two(x, axes, sizes, (a, 0))
            two = swap_two(x, axes, sizes, (0, b))
            both = swap_two(x, axes, sizes, (a, b))
            return x + one, two + both

        steps.append(square)
    steps += [lambda x, bit=bit: (x, swap(x, "col", groups, bit)) for bit in col_bits]
    while row_bits:
        (one, two), row_bits = (row_bits + [0])[:2], row_bits[2:]
        if two:
            steps.append(
                lambda x, one=one, two=two: (
                    x + swap(x, "row", row_size, one),
                    swap(x, "row", row_size, two) + swap(x, "row", row_size, one ^ two),
                )
            )
        else:
            steps.append(lambda x, one=one: (x, swap(x, "row", row_size, one)))
    for step in steps[:-1]:
        a, b = step(grad)
        grad = a + b
    return steps[-1](grad)


def local(row_size, groups, halves, adj_tiles, tile_rows, tile_cols, tile_counts, features_t, weight, bias_vec, cotangent):
    weights = [weight] + [shift(weight, "rep", halves, k) for k in range(1, halves)]
    pieces, (slabs, weights) = gather_row(features_t, row_size, (split_slabs(adj_tiles[0, 0]), weights))
    slot_info = (tile_rows, tile_cols, tile_counts)
    parts = mix((groups, halves), slot_info, slabs, pieces[:-1], pieces[-1:])

    terms = [None] * len(parts)
    for i in sorted(range(len(parts)), key=lambda i: -i):
        terms[i] = shift_two(parts[i], (groups, halves), divmod(i, halves)) if i else parts[i]
    output, *grads = node_step((groups, halves), terms, weights, bias_vec, cotangent)
    grad = grads[0]
    for k in range(1, halves):
        grad = grad + shift(grads[k], "rep", halves, -k)
    grad_weight, grad_bias = last_step(*sum_all(grad, groups, row_size))
    return output, grad_weight, grad_bias


def solution(mesh):
    row_size, groups, halves = (mesh.shape[axis] for axis in ("row", "col", "rep"))
    in_specs = (
        P("row", "col", None, None, None),
        P("row", "col", None),
        P("row", "col", None),
        P("row", "col"),
        P("rep", ("row", "col")),
        P("rep", None),
        P(),
        P(("row", "col", "rep"), None),
    )
    out_specs = (P(("row", "col", "rep"), None), P("rep", None), P())
    return jax.shard_map(
        functools.partial(local, row_size, groups, halves),
        mesh=mesh,
        in_specs=in_specs,
        out_specs=out_specs,
        check_vma=False,
    )
```

```python
import functools

import jax
import jax.numpy as jnp
from jax import lax
from jax.experimental import pallas as pl
from jax.experimental.pallas import tpu as pltpu
from jax.sharding import PartitionSpec as P

F32 = jnp.float32
BF16 = jnp.bfloat16
SUBLANES = 8
LANES = 128
VMEM_BYTES = 40 * 2**20


def dot(a, b, dims=((1,), (0,))):
    return lax.dot_general(a, b, (dims, ((), ())), preferred_element_type=F32)


def split(x):
    high = x.astype(BF16)
    return high, (x - high.astype(F32)).astype(BF16)


def dot_split(a, b, dims):
    (ah, al), (bh, bl) = a, b
    return dot(ah, bh, dims) + (dot(ah, bl, dims) + dot(al, bh, dims))


def call(kernel, out_shape, spaces, name, scratch=(), cost=None):
    return pl.pallas_call(
        kernel,
        out_shape=out_shape,
        in_specs=[pl.BlockSpec(memory_space=space) for space in spaces],
        out_specs=jax.tree.map(lambda _: pl.BlockSpec(memory_space=pltpu.VMEM), out_shape),
        scratch_shapes=list(scratch),
        compiler_params=pltpu.CompilerParams(vmem_limit_bytes=VMEM_BYTES),
        cost_estimate=cost,
        name=name,
    )


def split_kernel(sources, groups, slabs, rows, cols, high, low, plan, held, rows_s, cols_s, sems):
    slots = slabs.shape[0]
    copies = [pltpu.make_async_copy(slabs.at[t], held.at[t], sems.at[t]) for t in range(slots)]
    for k, pair in enumerate(((rows, rows_s), (cols, cols_s))):
        copies.append(pltpu.make_async_copy(*pair, sems.at[slots + k]))
    for copy in copies:
        copy.start()
    for copy in copies[slots:]:
        copy.wait()
    row = lax.axis_index("row")
    which = place = 0
    for t in range(slots):
        digit = 0
        for p, source in enumerate(sources):
            digit = jnp.where(cols_s[0, 0, t] == source(row), p + 1, digit)
        which = which * (len(sources) + 1) + digit
        place = place * groups + jnp.clip(rows_s[0, 0, t], 0, groups - 1)
    plan[0] = jnp.full(plan.shape[1:], which, jnp.int32)
    plan[1] = jnp.full(plan.shape[1:], place, jnp.int32)
    for t, copy in enumerate(copies[:slots]):
        copy.wait()
        high[t], low[t] = split(held[t].T)


def split_slabs(slabs, tile_rows, tile_cols, sources, groups):
    slots = slabs.shape[0]
    outs = [pltpu.VMEM(slabs.shape, BF16)] * 2 + [pltpu.VMEM((2, SUBLANES, LANES), jnp.int32)]
    scratch = [pltpu.VMEM(slabs.shape, F32)] + [pltpu.SMEM(tile_rows.shape, jnp.int32)] * 2
    scratch.append(pltpu.SemaphoreType.DMA((slots + 2,)))
    cost = pl.CostEstimate(flops=4 * slabs.size, bytes_accessed=8 * slabs.size, transcendentals=0)
    operands = [pltpu.with_memory_space_constraint(x, pltpu.HBM) for x in (slabs, tile_rows, tile_cols)]
    kernel = functools.partial(split_kernel, sources, groups)
    return call(kernel, outs, [pl.ANY] * len(operands), "split_slabs", scratch, cost)(*operands)


def digits(number, base, count):
    return [lax.rem(lax.div(number, base ** (count - 1 - t)), base) for t in range(count)]


def product(piece, high, low):
    half_width = piece.shape[0] // 2
    by_high = dot(piece, high)
    return by_high[:half_width] + by_high[half_width:] + dot(piece[:half_width], low)


def pick(picked, t, piece):
    half_width = piece.shape[0]
    picked[t, :half_width], picked[t, half_width:] = split(piece[...])


def early_kernel(bases, counts, plan, high, low, *refs):
    pieces, (total, rest, picked, which) = refs[:-4], refs[-4:]
    slots = high.shape[0]
    place = digits(plan[1][0, 0], bases[1], slots)
    found = [jnp.where(t < counts[0, 0], d, 0) for t, d in enumerate(digits(plan[0][0, 0], bases[0], slots))]
    left = 0
    for t in range(slots):
        which[t] = found[t]
        left = left * (bases[1] + 1) + jnp.where(found[t] > len(pieces), place[t] + 1, 0)
    rest[...] = jnp.full(rest.shape, left, jnp.int32)
    for p, piece in enumerate(pieces):

        @pl.loop(0, slots)
        def _(t):
            @pl.when(which[t] == p + 1)
            def _():
                pick(picked, t, piece)

    total[...] = jnp.zeros_like(total)
    for t in range(slots):

        @pl.when((found[t] > 0) & (found[t] <= len(pieces)))
        def _():
            total[place[t]] += product(picked[t], high[t], low[t])


def late_kernel(sizes, plan, high, low, early, piece, *refs):
    groups, halves = sizes
    outs, (total, picked) = refs[:-2], refs[-2:]
    slots = high.shape[0]
    block_len = early.shape[2]
    col, rep = lax.axis_index("col"), lax.axis_index("rep")
    place = digits(plan[...][0, 0], groups + 1, slots)
    total[...] = early[...]
    pick(picked, 0, piece)
    for t in range(slots):

        @pl.when(place[t] > 0)
        def _():
            total[place[t] - 1] += product(picked[0], high[t], low[t])

    part = block_len // halves
    for i, out in enumerate(outs):
        k, h = divmod(i, halves)
        begin = pl.multiple_of(lax.rem(rep + h, halves) * part, part)
        out[...] = total[lax.rem(col + k, groups), :, pl.ds(begin, part)]


def mix(sizes, slabs, counts, plan, pieces):
    groups, halves = sizes
    slots = slabs[0].shape[0]
    half_width, block_len = pieces[0].shape
    bases = (len(pieces) + 1, groups)
    picked = pltpu.VMEM((slots, 2 * half_width, block_len), BF16)
    total, rest = call(
        functools.partial(early_kernel, bases),
        [pltpu.VMEM((groups, half_width, block_len), F32), pltpu.VMEM((SUBLANES, LANES), jnp.int32)],
        [pltpu.SMEM] + [pltpu.VMEM] * (2 + len(pieces)),
        "mix_early",
        [picked, pltpu.SMEM((slots,), jnp.int32)],
        pl.CostEstimate(flops=6 * slabs[0].size * half_width, bytes_accessed=4 * slabs[0].size, transcendentals=0),
    )(counts, plan, *slabs, *pieces[:-1])
    return call(
        functools.partial(late_kernel, sizes),
        [pltpu.VMEM((half_width, block_len // halves), F32)] * (groups * halves),
        [pltpu.VMEM] * 5,
        "mix_late",
        [pltpu.VMEM(total.shape, F32), picked],
    )(rest, *slabs, total, pieces[-1])


def node_kernel(groups, halves, *refs):
    terms, refs = refs[: groups * halves], refs[groups * halves :]
    weights, (bias, cotangent, output, *grads) = refs[:halves], refs[halves:]
    half_width = terms[0].shape[0]
    mixed = [sum(terms[k * halves + h][...] for k in range(groups)) for h in range(halves)]
    mixed = split(jnp.concatenate(mixed))
    weight = split(jnp.concatenate([w[...] for w in weights]))
    preact = bias[...] + dot_split(mixed, weight, ((0,), (0,)))
    squash = 1.0 / (1.0 + jnp.exp(-preact))
    output[...] = preact * squash
    slope = cotangent[...] * squash * (1.0 + preact * (1.0 - squash))
    bias_term = jnp.sum(slope, axis=0, keepdims=True)
    product = dot_split(mixed, split(slope), ((1,), (0,)))
    for h, grad in enumerate(grads):
        grad[:half_width] = product[h * half_width : (h + 1) * half_width]
        grad[half_width:] = jnp.broadcast_to(bias_term, (SUBLANES, bias_term.shape[1]))


def node_step(sizes, terms, weights, bias, cotangent):
    groups, halves = sizes
    width = cotangent.shape[1]
    grad = pltpu.VMEM((terms[0].shape[0] + SUBLANES, width), F32)
    return call(
        functools.partial(node_kernel, groups, halves),
        [pltpu.VMEM(cotangent.shape, F32)] + [grad] * halves,
        [pltpu.VMEM] * (len(terms) + halves + 2),
        "node_step",
    )(*terms, *weights, bias.reshape(1, width), cotangent)


def last_kernel(a, b, grad_weight, grad_bias):
    half_width = grad_weight.shape[0]
    grad_weight[...] = a[:half_width] + b[:half_width]
    grad_bias[...] = a[half_width] + b[half_width]


def last_step(a, b):
    half_width, width = a.shape[0] - SUBLANES, a.shape[1]
    out = [jax.ShapeDtypeStruct((half_width, width), F32), jax.ShapeDtypeStruct((width,), F32)]
    return call(last_kernel, out, [pltpu.VMEM] * 2, "last_step")(a, b)


def shift(x, axis, size, k):
    return lax.ppermute(x, axis, [(i, (i + k) % size) for i in range(size)])


def shift_two(x, sizes, steps):
    (groups, halves), (k, h) = sizes, steps
    perm = [
        (c * halves + r, (c + k) % groups * halves + (r + h) % halves) for c in range(groups) for r in range(halves)
    ]
    return lax.ppermute(x, ("col", "rep"), perm)


def swap(x, axis, size, bit):
    return lax.ppermute(x, axis, [(i, i ^ bit) for i in range(size)])


def swap_two(x, axes, sizes, bits):
    (_, minor), perm = sizes, []
    for i in range(sizes[0]):
        for j in range(minor):
            perm.append((i * minor + j, (i ^ bits[0]) * minor + (j ^ bits[1])))
    return lax.ppermute(x, axes, perm)


def is_power(n):
    return n & (n - 1) == 0


def line_basis(size):
    bits = [1 << i for i in range(1, size.bit_length() - 1)]
    return [size - 2] + bits[-2::-1] if bits else []


def piece_sources(size):
    if not is_power(size) or size < 2:
        return [lambda row, k=k: lax.rem(row + size - k, size) for k in range(size)]
    return [lambda row, mask=mask: lax.bitwise_xor(row, mask) for mask in piece_masks(size)]


def piece_masks(size):
    lines = [0]
    for mask in line_basis(size):
        lines += [other ^ mask for other in lines]
    last = max(lines, key=lambda mask: (lines.index(mask) > 0 and mask not in line_basis(size), lines.index(mask)))
    crossed = [mask ^ 1 for mask in lines if mask != last] + [last ^ 1]
    return lines + crossed


def gather_row(x, size, held):
    if not is_power(size) or size < 2:
        return [x] + [shift(x, "row", size, k) for k in range(1, size)], held
    basis = line_basis(size)
    own_cross = swap(x, "row", size, 1)
    pieces = {0: x, 1: own_cross}
    if len(basis) > 1:
        pieces[basis[-1] ^ 1] = swap(x, "row", size, basis[-1] ^ 1)
    lines = [0]
    for step, mask in enumerate(basis):
        for other in lines:
            if step and step == len(basis) - 1 and not other:
                free, _ = lax.optimization_barrier((x, pieces[mask ^ 1]))
                pieces[mask] = swap(free, "row", size, mask)
            else:
                pieces[other ^ mask] = swap(pieces[other], "row", size, mask)
        if step == 0:
            pieces[mask], pieces[1], held = lax.optimization_barrier((pieces[mask], pieces[1], held))
        lines += [other ^ mask for other in lines]
    order = piece_masks(size)
    for mask in lines:
        if mask ^ 1 not in pieces:
            block = pieces[mask]
            if mask ^ 1 == order[-1] and len(basis) > 1:
                block, _ = lax.optimization_barrier((block, pieces[basis[-1] ^ 1]))
            pieces[mask ^ 1] = swap(block, "row", size, 1)
    return [pieces[mask] for mask in order], held


def sum_all(grad, groups, row_size):
    if not (is_power(groups) and is_power(row_size)) or groups * row_size == 1:
        grad = lax.psum(grad, ("row", "col"))
        return grad, jnp.zeros_like(grad)
    col_bits = [1 << i for i in range(groups.bit_length() - 1)]
    row_bits = [1 << i for i in range(row_size.bit_length() - 1)]
    steps = []
    if col_bits and row_bits:
        axes, sizes, a, b = ("row", "col"), (row_size, groups), row_bits.pop(0), col_bits.pop(0)

        def square(x):
            one = swap_two(x, axes, sizes, (a, 0))
            two = swap_two(x, axes, sizes, (0, b))
            both = swap_two(x, axes, sizes, (a, b))
            return x + one, two + both

        steps.append(square)
    steps += [lambda x, bit=bit: (x, swap(x, "col", groups, bit)) for bit in col_bits]
    while row_bits:
        (one, two), row_bits = (row_bits + [0])[:2], row_bits[2:]
        if two:
            steps.append(
                lambda x, one=one, two=two: (
                    x + swap(x, "row", row_size, one),
                    swap(x, "row", row_size, two) + swap(x, "row", row_size, one ^ two),
                )
            )
        else:
            steps.append(lambda x, one=one: (x, swap(x, "row", row_size, one)))
    for step in steps[:-1]:
        a, b = step(grad)
        grad = a + b
    return steps[-1](grad)


def local(row_size, groups, halves, adj_tiles, tile_rows, tile_cols, tile_counts, features_t, weight, bias_vec, cotangent):
    weights = [weight] + [shift(weight, "rep", halves, k) for k in range(1, halves)]
    *slabs, plan = split_slabs(adj_tiles[0, 0], tile_rows, tile_cols, piece_sources(row_size), groups)
    pieces, (slabs, plan, weights) = gather_row(features_t, row_size, (slabs, plan, weights))
    parts = mix((groups, halves), slabs, tile_counts, plan, pieces)

    terms = [None] * len(parts)
    for i in sorted(range(len(parts)), key=lambda i: -i):
        terms[i] = shift_two(parts[i], (groups, halves), divmod(i, halves)) if i else parts[i]
    output, *grads = node_step((groups, halves), terms, weights, bias_vec, cotangent)
    grad = grads[0]
    for k in range(1, halves):
        grad = grad + shift(grads[k], "rep", halves, -k)
    grad_weight, grad_bias = last_step(*sum_all(grad, groups, row_size))
    return output, grad_weight, grad_bias


def solution(mesh):
    row_size, groups, halves = (mesh.shape[axis] for axis in ("row", "col", "rep"))
    in_specs = (
        P("row", "col", None, None, None),
        P("row", "col", None),
        P("row", "col", None),
        P("row", "col"),
        P("rep", ("row", "col")),
        P("rep", None),
        P(),
        P(("row", "col", "rep"), None),
    )
    out_specs = (P(("row", "col", "rep"), None), P("rep", None), P())
    return jax.shard_map(
        functools.partial(local, row_size, groups, halves),
        mesh=mesh,
        in_specs=in_specs,
        out_specs=out_specs,
        check_vma=False,
    )
```

```python
import functools

import jax
import jax.numpy as jnp
from jax import lax
from jax.experimental import pallas as pl
from jax.experimental.pallas import tpu as pltpu
from jax.sharding import PartitionSpec as P

F32 = jnp.float32
BF16 = jnp.bfloat16
SUBLANES = 8
LANES = 128
VMEM_BYTES = 40 * 2**20


def dot(a, b, dims=((1,), (0,))):
    return lax.dot_general(a, b, (dims, ((), ())), preferred_element_type=F32)


def split(x):
    high = x.astype(BF16)
    return high, (x - high.astype(F32)).astype(BF16)


def dot_split(a, b, dims):
    (ah, al), (bh, bl) = a, b
    return dot(ah, bh, dims) + (dot(ah, bl, dims) + dot(al, bh, dims))


def call(kernel, out_shape, spaces, name, scratch=(), cost=None):
    return pl.pallas_call(
        kernel,
        out_shape=out_shape,
        in_specs=[pl.BlockSpec(memory_space=space) for space in spaces],
        out_specs=jax.tree.map(lambda _: pl.BlockSpec(memory_space=pltpu.VMEM), out_shape),
        scratch_shapes=list(scratch),
        compiler_params=pltpu.CompilerParams(vmem_limit_bytes=VMEM_BYTES),
        cost_estimate=cost,
        name=name,
    )


def split_kernel(sources, groups, slabs, rows, cols, high, low, plan, held, rows_s, cols_s, sems):
    slots = slabs.shape[0]
    copies = [pltpu.make_async_copy(slabs.at[t], held.at[t], sems.at[t]) for t in range(slots)]
    for k, pair in enumerate(((rows, rows_s), (cols, cols_s))):
        copies.append(pltpu.make_async_copy(*pair, sems.at[slots + k]))
    for copy in copies:
        copy.start()
    for copy in copies[slots:]:
        copy.wait()
    row = lax.axis_index("row")
    which = place = 0
    for t in range(slots):
        digit = 0
        for p, source in enumerate(sources):
            digit = jnp.where(cols_s[0, 0, t] == source(row), p + 1, digit)
        which = which * (len(sources) + 1) + digit
        place = place * groups + jnp.clip(rows_s[0, 0, t], 0, groups - 1)
    plan[0] = jnp.full(plan.shape[1:], which, jnp.int32)
    plan[1] = jnp.full(plan.shape[1:], place, jnp.int32)
    for t, copy in enumerate(copies[:slots]):
        copy.wait()
        high[t], low[t] = split(held[t].T)


def split_slabs(slabs, tile_rows, tile_cols, sources, groups):
    slots = slabs.shape[0]
    outs = [pltpu.VMEM(slabs.shape, BF16)] * 2 + [pltpu.VMEM((2, SUBLANES, LANES), jnp.int32)]
    scratch = [pltpu.VMEM(slabs.shape, F32)] + [pltpu.SMEM(tile_rows.shape, jnp.int32)] * 2
    scratch.append(pltpu.SemaphoreType.DMA((slots + 2,)))
    cost = pl.CostEstimate(flops=4 * slabs.size, bytes_accessed=8 * slabs.size, transcendentals=0)
    operands = [pltpu.with_memory_space_constraint(x, pltpu.HBM) for x in (slabs, tile_rows, tile_cols)]
    kernel = functools.partial(split_kernel, sources, groups)
    return call(kernel, outs, [pl.ANY] * len(operands), "split_slabs", scratch, cost)(*operands)


def digits(number, base, count):
    return [lax.rem(lax.div(number, base ** (count - 1 - t)), base) for t in range(count)]


def product(piece, high, low):
    half_width = piece.shape[0] // 2
    by_high = dot(piece, high)
    return by_high[:half_width] + by_high[half_width:] + dot(piece[:half_width], low)


def pick(picked, t, piece):
    half_width = piece.shape[0]
    picked[t, :half_width], picked[t, half_width:] = split(piece[...])


def early_kernel(bases, counts, plan, high, low, *refs):
    pieces, (total, rest, picked, which) = refs[:-4], refs[-4:]
    slots = high.shape[0]
    place = digits(plan[1][0, 0], bases[1], slots)
    found = [jnp.where(t < counts[0, 0], d, 0) for t, d in enumerate(digits(plan[0][0, 0], bases[0], slots))]
    left = 0
    for t in range(slots):
        which[t] = found[t]
        left = left * (bases[1] + 1) + jnp.where(found[t] > len(pieces), place[t] + 1, 0)
    rest[...] = jnp.full(rest.shape, left, jnp.int32)
    for p, piece in enumerate(pieces):

        @pl.loop(0, slots)
        def _(t):
            @pl.when(which[t] == p + 1)
            def _():
                pick(picked, t, piece)

    total[...] = jnp.zeros_like(total)
    for t in range(slots):

        @pl.when((found[t] > 0) & (found[t] <= len(pieces)))
        def _():
            total[place[t]] += product(picked[t], high[t], low[t])


def late_kernel(sizes, plan, high, low, early, piece, *refs):
    groups, halves = sizes
    outs, (total, picked) = refs[:-2], refs[-2:]
    slots = high.shape[0]
    block_len = early.shape[2]
    col, rep = lax.axis_index("col"), lax.axis_index("rep")
    place = digits(plan[...][0, 0], groups + 1, slots)
    total[...] = early[...]
    pick(picked, 0, piece)
    for t in range(slots):

        @pl.when(place[t] > 0)
        def _():
            total[place[t] - 1] += product(picked[0], high[t], low[t])

    part = block_len // halves
    for i, out in enumerate(outs):
        k, h = divmod(i, halves)
        begin = pl.multiple_of(lax.rem(rep + h, halves) * part, part)
        out[...] = total[lax.rem(col + k, groups), :, pl.ds(begin, part)]


def mix(sizes, slabs, counts, plan, pieces):
    groups, halves = sizes
    slots = slabs[0].shape[0]
    half_width, block_len = pieces[0].shape
    bases = (len(pieces) + 1, groups)
    picked = pltpu.VMEM((slots, 2 * half_width, block_len), BF16)
    total, rest = call(
        functools.partial(early_kernel, bases),
        [pltpu.VMEM((groups, half_width, block_len), F32), pltpu.VMEM((SUBLANES, LANES), jnp.int32)],
        [pltpu.SMEM] + [pltpu.VMEM] * (2 + len(pieces)),
        "mix_early",
        [picked, pltpu.SMEM((slots,), jnp.int32)],
        pl.CostEstimate(flops=6 * slabs[0].size * half_width, bytes_accessed=4 * slabs[0].size, transcendentals=0),
    )(counts, plan, *slabs, *pieces[:-1])
    return call(
        functools.partial(late_kernel, sizes),
        [pltpu.VMEM((half_width, block_len // halves), F32)] * (groups * halves),
        [pltpu.VMEM] * 5,
        "mix_late",
        [pltpu.VMEM(total.shape, F32), picked],
    )(rest, *slabs, total, pieces[-1])


def node_kernel(groups, halves, *refs):
    terms, refs = refs[: groups * halves], refs[groups * halves :]
    weights, (bias, cotangent, output, *grads) = refs[:halves], refs[halves:]
    half_width = terms[0].shape[0]
    mixed = [sum(terms[k * halves + h][...] for k in range(groups)) for h in range(halves)]
    mixed = split(jnp.concatenate(mixed))
    weight = split(jnp.concatenate([w[...] for w in weights]))
    preact = bias[...] + dot_split(mixed, weight, ((0,), (0,)))
    squash = 1.0 / (1.0 + jnp.exp(-preact))
    output[...] = preact * squash
    slope = cotangent[...] * squash * (1.0 + preact * (1.0 - squash))
    bias_term = jnp.sum(slope, axis=0, keepdims=True)
    product = dot_split(mixed, split(slope), ((1,), (0,)))
    for h, grad in enumerate(grads):
        grad[:half_width] = product[h * half_width : (h + 1) * half_width]
        grad[half_width:] = jnp.broadcast_to(bias_term, (SUBLANES, bias_term.shape[1]))


def node_step(sizes, terms, weights, bias, cotangent):
    groups, halves = sizes
    width = cotangent.shape[1]
    grad = pltpu.VMEM((terms[0].shape[0] + SUBLANES, width), F32)
    return call(
        functools.partial(node_kernel, groups, halves),
        [pltpu.VMEM(cotangent.shape, F32)] + [grad] * halves,
        [pltpu.VMEM] * (len(terms) + halves + 2),
        "node_step",
    )(*terms, *weights, bias.reshape(1, width), cotangent)


def last_kernel(a, b, grad_weight, grad_bias):
    half_width = grad_weight.shape[0]
    grad_weight[...] = a[:half_width] + b[:half_width]
    grad_bias[...] = a[half_width] + b[half_width]


def last_step(a, b):
    half_width, width = a.shape[0] - SUBLANES, a.shape[1]
    out = [jax.ShapeDtypeStruct((half_width, width), F32), jax.ShapeDtypeStruct((width,), F32)]
    return call(last_kernel, out, [pltpu.VMEM] * 2, "last_step")(a, b)


def shift(x, axis, size, k):
    return lax.ppermute(x, axis, [(i, (i + k) % size) for i in range(size)])


def shift_two(x, sizes, steps):
    (groups, halves), (k, h) = sizes, steps
    perm = [
        (c * halves + r, (c + k) % groups * halves + (r + h) % halves) for c in range(groups) for r in range(halves)
    ]
    return lax.ppermute(x, ("col", "rep"), perm)


def swap(x, axis, size, bit):
    return lax.ppermute(x, axis, [(i, i ^ bit) for i in range(size)])


def swap_two(x, axes, sizes, bits):
    (_, minor), perm = sizes, []
    for i in range(sizes[0]):
        for j in range(minor):
            perm.append((i * minor + j, (i ^ bits[0]) * minor + (j ^ bits[1])))
    return lax.ppermute(x, axes, perm)


def is_power(n):
    return n & (n - 1) == 0


def line_basis(size):
    bits = [1 << i for i in range(1, size.bit_length() - 1)]
    return [size - 2] + bits[-2::-1] if bits else []


def piece_sources(size):
    if not is_power(size) or size < 2:
        return [lambda row, k=k: lax.rem(row + size - k, size) for k in range(size)]
    return [lambda row, mask=mask: lax.bitwise_xor(row, mask) for mask in piece_masks(size)]


def piece_masks(size):
    lines = [0]
    for mask in line_basis(size):
        lines += [other ^ mask for other in lines]
    last = max(lines, key=lambda mask: (lines.index(mask) > 0 and mask not in line_basis(size), lines.index(mask)))
    crossed = [mask ^ 1 for mask in lines if mask != last] + [last ^ 1]
    return lines + crossed


def gather_row(x, size, held):
    if not is_power(size) or size < 2:
        return [x] + [shift(x, "row", size, k) for k in range(1, size)], held
    basis = line_basis(size)
    own_cross = swap(x, "row", size, 1)
    pieces = {0: x, 1: own_cross}
    if len(basis) > 1:
        pieces[basis[-1] ^ 1] = swap(x, "row", size, basis[-1] ^ 1)
    lines = [0]
    for step, mask in enumerate(basis):
        for other in lines:
            if step and step == len(basis) - 1 and not other:
                free, _ = lax.optimization_barrier((x, pieces[mask ^ 1]))
                pieces[mask] = swap(free, "row", size, mask)
            else:
                pieces[other ^ mask] = swap(pieces[other], "row", size, mask)
        if step == 0:
            pieces[mask], pieces[1], held = lax.optimization_barrier((pieces[mask], pieces[1], held))
        lines += [other ^ mask for other in lines]
    order = piece_masks(size)
    for mask in lines:
        if mask ^ 1 not in pieces:
            block = pieces[mask]
            if mask ^ 1 == order[-1] and len(basis) > 1:
                block, _ = lax.optimization_barrier((block, pieces[basis[-1] ^ 1]))
            pieces[mask ^ 1] = swap(block, "row", size, 1)
    return [pieces[mask] for mask in order], held


def sum_all(grad, groups, row_size):
    if not (is_power(groups) and is_power(row_size)) or groups * row_size == 1:
        grad = lax.psum(grad, ("row", "col"))
        return grad, jnp.zeros_like(grad)
    col_bits = [1 << i for i in range(groups.bit_length() - 1)]
    row_bits = [1 << i for i in range(row_size.bit_length() - 1)]
    steps = []
    if col_bits and row_bits:
        axes, sizes, a, b = ("row", "col"), (row_size, groups), row_bits.pop(0), col_bits.pop(0)

        def square(x):
            one = swap_two(x, axes, sizes, (a, 0))
            two = swap_two(x, axes, sizes, (0, b))
            both = swap_two(x, axes, sizes, (a, b))
            return x + one, two + both

        steps.append(square)
    steps += [lambda x, bit=bit: (x, swap(x, "col", groups, bit)) for bit in col_bits]
    while row_bits:
        (one, two), row_bits = (row_bits + [0])[:2], row_bits[2:]
        if two:
            steps.append(
                lambda x, one=one, two=two: (
                    x + swap(x, "row", row_size, one ^ two),
                    swap(x, "row", row_size, two) + swap(x, "row", row_size, one),
                )
            )
        else:
            steps.append(lambda x, one=one: (x, swap(x, "row", row_size, one)))
    for step in steps[:-1]:
        a, b = step(grad)
        grad = a + b
    return steps[-1](grad)


def local(row_size, groups, halves, adj_tiles, tile_rows, tile_cols, tile_counts, features_t, weight, bias_vec, cotangent):
    weights = [weight] + [shift(weight, "rep", halves, k) for k in range(1, halves)]
    *slabs, plan = split_slabs(adj_tiles[0, 0], tile_rows, tile_cols, piece_sources(row_size), groups)
    pieces, (slabs, plan, weights) = gather_row(features_t, row_size, (slabs, plan, weights))
    parts = mix((groups, halves), slabs, tile_counts, plan, pieces)

    terms = [None] * len(parts)
    for i in sorted(range(len(parts)), key=lambda i: -i):
        terms[i] = shift_two(parts[i], (groups, halves), divmod(i, halves)) if i else parts[i]
    output, *grads = node_step((groups, halves), terms, weights, bias_vec, cotangent)
    grad = grads[0]
    for k in range(1, halves):
        grad = grad + shift(grads[k], "rep", halves, -k)
    grad_weight, grad_bias = last_step(*sum_all(grad, groups, row_size))
    return output, grad_weight, grad_bias


def solution(mesh):
    row_size, groups, halves = (mesh.shape[axis] for axis in ("row", "col", "rep"))
    in_specs = (
        P("row", "col", None, None, None),
        P("row", "col", None),
        P("row", "col", None),
        P("row", "col"),
        P("rep", ("row", "col")),
        P("rep", None),
        P(),
        P(("row", "col", "rep"), None),
    )
    out_specs = (P(("row", "col", "rep"), None), P("rep", None), P())
    return jax.shard_map(
        functools.partial(local, row_size, groups, halves),
        mesh=mesh,
        in_specs=in_specs,
        out_specs=out_specs,
        check_vma=False,
    )
```

```python
import functools

import jax
import jax.numpy as jnp
from jax import lax
from jax.experimental import pallas as pl
from jax.experimental.pallas import tpu as pltpu
from jax.sharding import PartitionSpec as P

F32 = jnp.float32
BF16 = jnp.bfloat16
SUBLANES = 8
LANES = 128
VMEM_BYTES = 40 * 2**20


def dot(a, b, dims=((1,), (0,))):
    return lax.dot_general(a, b, (dims, ((), ())), preferred_element_type=F32)


def split(x):
    high = x.astype(BF16)
    return high, (x - high.astype(F32)).astype(BF16)


def dot_split(a, b, dims):
    (ah, al), (bh, bl) = a, b
    return dot(ah, bh, dims) + (dot(ah, bl, dims) + dot(al, bh, dims))


def call(kernel, out_shape, spaces, name, scratch=(), cost=None):
    return pl.pallas_call(
        kernel,
        out_shape=out_shape,
        in_specs=[pl.BlockSpec(memory_space=space) for space in spaces],
        out_specs=jax.tree.map(lambda _: pl.BlockSpec(memory_space=pltpu.VMEM), out_shape),
        scratch_shapes=list(scratch),
        compiler_params=pltpu.CompilerParams(vmem_limit_bytes=VMEM_BYTES),
        cost_estimate=cost,
        name=name,
    )


def split_kernel(sources, groups, slabs, rows, cols, high, low, plan, held, rows_s, cols_s, sems):
    slots = slabs.shape[0]
    copies = [pltpu.make_async_copy(slabs.at[t], held.at[t], sems.at[t]) for t in range(slots)]
    for k, pair in enumerate(((rows, rows_s), (cols, cols_s))):
        copies.append(pltpu.make_async_copy(*pair, sems.at[slots + k]))
    for copy in copies:
        copy.start()
    for copy in copies[slots:]:
        copy.wait()
    row = lax.axis_index("row")
    which = place = 0
    for t in range(slots):
        digit = 0
        for p, source in enumerate(sources):
            digit = jnp.where(cols_s[0, 0, t] == source(row), p + 1, digit)
        which = which * (len(sources) + 1) + digit
        place = place * groups + jnp.clip(rows_s[0, 0, t], 0, groups - 1)
    plan[0] = jnp.full(plan.shape[1:], which, jnp.int32)
    plan[1] = jnp.full(plan.shape[1:], place, jnp.int32)
    for t, copy in enumerate(copies[:slots]):
        copy.wait()
        high[t], low[t] = split(held[t].T)


def split_slabs(slabs, tile_rows, tile_cols, sources, groups):
    slots = slabs.shape[0]
    outs = [pltpu.VMEM(slabs.shape, BF16)] * 2 + [pltpu.VMEM((2, SUBLANES, LANES), jnp.int32)]
    scratch = [pltpu.VMEM(slabs.shape, F32)] + [pltpu.SMEM(tile_rows.shape, jnp.int32)] * 2
    scratch.append(pltpu.SemaphoreType.DMA((slots + 2,)))
    cost = pl.CostEstimate(flops=4 * slabs.size, bytes_accessed=8 * slabs.size, transcendentals=0)
    operands = [pltpu.with_memory_space_constraint(x, pltpu.HBM) for x in (slabs, tile_rows, tile_cols)]
    kernel = functools.partial(split_kernel, sources, groups)
    return call(kernel, outs, [pl.ANY] * len(operands), "split_slabs", scratch, cost)(*operands)


def digits(number, base, count):
    return [lax.rem(lax.div(number, base ** (count - 1 - t)), base) for t in range(count)]


def product(piece, high, low):
    half_width = piece.shape[0] // 2
    by_high = dot(piece, high)
    return by_high[:half_width] + by_high[half_width:] + dot(piece[:half_width], low)


def pick(picked, t, piece):
    half_width = piece.shape[0]
    picked[t, :half_width], picked[t, half_width:] = split(piece[...])


def early_kernel(bases, counts, plan, high, low, *refs):
    pieces, (total, rest, picked, which) = refs[:-4], refs[-4:]
    slots = high.shape[0]
    place = digits(plan[1][0, 0], bases[1], slots)
    found = [jnp.where(t < counts[0, 0], d, 0) for t, d in enumerate(digits(plan[0][0, 0], bases[0], slots))]
    left = 0
    for t in range(slots):
        which[t] = found[t]
        left = left * (bases[1] + 1) + jnp.where(found[t] > len(pieces), place[t] + 1, 0)
    rest[...] = jnp.full(rest.shape, left, jnp.int32)
    for p, piece in enumerate(pieces):

        @pl.loop(0, slots)
        def _(t):
            @pl.when(which[t] == p + 1)
            def _():
                pick(picked, t, piece)

    total[...] = jnp.zeros_like(total)
    for t in range(slots):

        @pl.when((found[t] > 0) & (found[t] <= len(pieces)))
        def _():
            total[place[t]] += product(picked[t], high[t], low[t])


def late_kernel(sizes, plan, high, low, early, piece, *refs):
    groups, halves = sizes
    outs, (total, picked) = refs[:-2], refs[-2:]
    slots = high.shape[0]
    block_len = early.shape[2]
    col, rep = lax.axis_index("col"), lax.axis_index("rep")
    place = digits(plan[...][0, 0], groups + 1, slots)
    total[...] = early[...]
    pick(picked, 0, piece)
    for t in range(slots):

        @pl.when(place[t] > 0)
        def _():
            total[place[t] - 1] += product(picked[0], high[t], low[t])

    part = block_len // halves
    for i, out in enumerate(outs):
        k, h = divmod(i, halves)
        begin = pl.multiple_of(lax.rem(rep + h, halves) * part, part)
        out[...] = total[lax.rem(col + k, groups), :, pl.ds(begin, part)]


def mix(sizes, slabs, counts, plan, pieces):
    groups, halves = sizes
    slots = slabs[0].shape[0]
    half_width, block_len = pieces[0].shape
    bases = (len(pieces) + 1, groups)
    picked = pltpu.VMEM((slots, 2 * half_width, block_len), BF16)
    total, rest = call(
        functools.partial(early_kernel, bases),
        [pltpu.VMEM((groups, half_width, block_len), F32), pltpu.VMEM((SUBLANES, LANES), jnp.int32)],
        [pltpu.SMEM] + [pltpu.VMEM] * (2 + len(pieces)),
        "mix_early",
        [picked, pltpu.SMEM((slots,), jnp.int32)],
        pl.CostEstimate(flops=6 * slabs[0].size * half_width, bytes_accessed=4 * slabs[0].size, transcendentals=0),
    )(counts, plan, *slabs, *pieces[:-1])
    return call(
        functools.partial(late_kernel, sizes),
        [pltpu.VMEM((half_width, block_len // halves), F32)] * (groups * halves),
        [pltpu.VMEM] * 5,
        "mix_late",
        [pltpu.VMEM(total.shape, F32), picked],
    )(rest, *slabs, total, pieces[-1])


def node_kernel(groups, halves, *refs):
    terms, refs = refs[: groups * halves][::-1], refs[groups * halves :]
    weights, (bias, cotangent, output, *grads) = refs[:halves], refs[halves:]
    half_width = terms[0].shape[0]
    mixed = [sum(terms[k * halves + h][...] for k in range(groups)) for h in range(halves)]
    mixed = split(jnp.concatenate(mixed))
    weight = split(jnp.concatenate([w[...] for w in weights]))
    preact = bias[...] + dot_split(mixed, weight, ((0,), (0,)))
    squash = 1.0 / (1.0 + jnp.exp(-preact))
    output[...] = preact * squash
    slope = cotangent[...] * squash * (1.0 + preact * (1.0 - squash))
    bias_term = jnp.sum(slope, axis=0, keepdims=True)
    product = dot_split(mixed, split(slope), ((1,), (0,)))
    for h, grad in enumerate(grads):
        grad[:half_width] = product[h * half_width : (h + 1) * half_width]
        grad[half_width:] = jnp.broadcast_to(bias_term, (SUBLANES, bias_term.shape[1]))


def node_step(sizes, terms, weights, bias, cotangent):
    groups, halves = sizes
    width = cotangent.shape[1]
    grad = pltpu.VMEM((terms[0].shape[0] + SUBLANES, width), F32)
    return call(
        functools.partial(node_kernel, groups, halves),
        [pltpu.VMEM(cotangent.shape, F32)] + [grad] * halves,
        [pltpu.VMEM] * (len(terms) + halves + 2),
        "node_step",
    )(*terms[::-1], *weights, bias.reshape(1, width), cotangent)


def last_kernel(a, b, grad_weight, grad_bias):
    half_width = grad_weight.shape[0]
    grad_weight[...] = a[:half_width] + b[:half_width]
    grad_bias[...] = a[half_width] + b[half_width]


def last_step(a, b):
    half_width, width = a.shape[0] - SUBLANES, a.shape[1]
    out = [jax.ShapeDtypeStruct((half_width, width), F32), jax.ShapeDtypeStruct((width,), F32)]
    return call(last_kernel, out, [pltpu.VMEM] * 2, "last_step")(a, b)


def shift(x, axis, size, k):
    return lax.ppermute(x, axis, [(i, (i + k) % size) for i in range(size)])


def shift_two(x, sizes, steps):
    (groups, halves), (k, h) = sizes, steps
    perm = [
        (c * halves + r, (c + k) % groups * halves + (r + h) % halves) for c in range(groups) for r in range(halves)
    ]
    return lax.ppermute(x, ("col", "rep"), perm)


def swap(x, axis, size, bit):
    return lax.ppermute(x, axis, [(i, i ^ bit) for i in range(size)])


def swap_two(x, axes, sizes, bits):
    (_, minor), perm = sizes, []
    for i in range(sizes[0]):
        for j in range(minor):
            perm.append((i * minor + j, (i ^ bits[0]) * minor + (j ^ bits[1])))
    return lax.ppermute(x, axes, perm)


def is_power(n):
    return n & (n - 1) == 0


def line_basis(size):
    bits = [1 << i for i in range(1, size.bit_length() - 1)]
    return [size - 2] + bits[-2::-1] if bits else []


def piece_sources(size):
    if not is_power(size) or size < 2:
        return [lambda row, k=k: lax.rem(row + size - k, size) for k in range(size)]
    return [lambda row, mask=mask: lax.bitwise_xor(row, mask) for mask in piece_masks(size)]


def piece_masks(size):
    lines = [0]
    for mask in line_basis(size):
        lines += [other ^ mask for other in lines]
    last = max(lines, key=lambda mask: (lines.index(mask) > 0 and mask not in line_basis(size), lines.index(mask)))
    crossed = [mask ^ 1 for mask in lines if mask != last] + [last ^ 1]
    return lines + crossed


def gather_row(x, size, held):
    if not is_power(size) or size < 2:
        return [x] + [shift(x, "row", size, k) for k in range(1, size)], held
    basis = line_basis(size)
    own_cross = swap(x, "row", size, 1)
    pieces = {0: x, 1: own_cross}
    if len(basis) > 1:
        pieces[basis[-1] ^ 1] = swap(x, "row", size, basis[-1] ^ 1)
    lines = [0]
    for step, mask in enumerate(basis):
        for other in lines:
            if step and step == len(basis) - 1 and not other:
                free, _ = lax.optimization_barrier((x, pieces[mask ^ 1]))
                pieces[mask] = swap(free, "row", size, mask)
            else:
                pieces[other ^ mask] = swap(pieces[other], "row", size, mask)
        if step == 0:
            pieces[mask], pieces[1], held = lax.optimization_barrier((pieces[mask], pieces[1], held))
        lines += [other ^ mask for other in lines]
    order = piece_masks(size)
    for mask in lines:
        if mask ^ 1 not in pieces:
            block = pieces[mask]
            if mask ^ 1 == order[-1] and len(basis) > 1:
                block, _ = lax.optimization_barrier((block, pieces[basis[-1] ^ 1]))
            pieces[mask ^ 1] = swap(block, "row", size, 1)
    return [pieces[mask] for mask in order], held


def sum_all(grad, groups, row_size):
    if not (is_power(groups) and is_power(row_size)) or groups * row_size == 1:
        grad = lax.psum(grad, ("row", "col"))
        return grad, jnp.zeros_like(grad)
    col_bits = [1 << i for i in range(groups.bit_length() - 1)]
    row_bits = [1 << i for i in range(row_size.bit_length() - 1)]
    steps = []
    if col_bits and row_bits:
        axes, sizes, a, b = ("row", "col"), (row_size, groups), row_bits.pop(0), col_bits.pop(0)

        def square(x):
            one = swap_two(x, axes, sizes, (a, 0))
            two = swap_two(x, axes, sizes, (0, b))
            both = swap_two(x, axes, sizes, (a, b))
            return x + one, two + both

        steps.append(square)
    steps += [lambda x, bit=bit: (x, swap(x, "col", groups, bit)) for bit in col_bits]
    while row_bits:
        (one, two), row_bits = (row_bits + [0])[:2], row_bits[2:]
        if two:
            steps.append(
                lambda x, one=one, two=two: (
                    x + swap(x, "row", row_size, one ^ two),
                    swap(x, "row", row_size, two) + swap(x, "row", row_size, one),
                )
            )
        else:
            steps.append(lambda x, one=one: (x, swap(x, "row", row_size, one)))
    for step in steps[:-1]:
        terms = step(grad)
        grad = terms[0] + terms[1]
    return steps[-1](grad)


def local(row_size, groups, halves, adj_tiles, tile_rows, tile_cols, tile_counts, features_t, weight, bias_vec, cotangent):
    weights = [weight] + [shift(weight, "rep", halves, k) for k in range(1, halves)]
    *slabs, plan = split_slabs(adj_tiles[0, 0], tile_rows, tile_cols, piece_sources(row_size), groups)
    pieces, (slabs, plan, weights) = gather_row(features_t, row_size, (slabs, plan, weights))
    parts = mix((groups, halves), slabs, tile_counts, plan, pieces)

    terms = [None] * len(parts)
    for i in sorted(range(len(parts)), key=lambda i: -i):
        terms[i] = shift_two(parts[i], (groups, halves), divmod(i, halves)) if i else parts[i]
    output, *grads = node_step((groups, halves), terms, weights, bias_vec, cotangent)
    grad = grads[0]
    for k in range(1, halves):
        grad = grad + shift(grads[k], "rep", halves, -k)
    grad_weight, grad_bias = last_step(*sum_all(grad, groups, row_size))
    return output, grad_weight, grad_bias


def solution(mesh):
    row_size, groups, halves = (mesh.shape[axis] for axis in ("row", "col", "rep"))
    in_specs = (
        P("row", "col", None, None, None),
        P("row", "col", None),
        P("row", "col", None),
        P("row", "col"),
        P("rep", ("row", "col")),
        P("rep", None),
        P(),
        P(("row", "col", "rep"), None),
    )
    out_specs = (P(("row", "col", "rep"), None), P("rep", None), P())
    return jax.shard_map(
        functools.partial(local, row_size, groups, halves),
        mesh=mesh,
        in_specs=in_specs,
        out_specs=out_specs,
        check_vma=False,
    )
```

```python
import functools

import jax
import jax.numpy as jnp
from jax import lax
from jax.experimental import pallas as pl
from jax.experimental.pallas import tpu as pltpu
from jax.sharding import PartitionSpec as P

F32 = jnp.float32
BF16 = jnp.bfloat16
SUBLANES = 8
LANES = 128
VMEM_BYTES = 40 * 2**20


def dot(a, b, dims=((1,), (0,))):
    return lax.dot_general(a, b, (dims, ((), ())), preferred_element_type=F32)


def split(x):
    high = x.astype(BF16)
    return high, (x - high.astype(F32)).astype(BF16)


def dot_split(a, b, dims):
    (ah, al), (bh, bl) = a, b
    return dot(ah, bh, dims) + (dot(ah, bl, dims) + dot(al, bh, dims))


def call(kernel, out_shape, spaces, name, scratch=(), cost=None):
    return pl.pallas_call(
        kernel,
        out_shape=out_shape,
        in_specs=[pl.BlockSpec(memory_space=space) for space in spaces],
        out_specs=jax.tree.map(lambda _: pl.BlockSpec(memory_space=pltpu.VMEM), out_shape),
        scratch_shapes=list(scratch),
        compiler_params=pltpu.CompilerParams(vmem_limit_bytes=VMEM_BYTES),
        cost_estimate=cost,
        name=name,
    )


def split_kernel(sources, groups, slabs, rows, cols, high, low, plan, held, rows_s, cols_s, sems):
    slots = slabs.shape[0]
    copies = [pltpu.make_async_copy(slabs.at[t], held.at[t], sems.at[t]) for t in range(slots)]
    for k, pair in enumerate(((rows, rows_s), (cols, cols_s))):
        copies.append(pltpu.make_async_copy(*pair, sems.at[slots + k]))
    for copy in copies:
        copy.start()
    for copy in copies[slots:]:
        copy.wait()
    row = lax.axis_index("row")
    which = place = 0
    for t in range(slots):
        digit = 0
        for p, source in enumerate(sources):
            digit = jnp.where(cols_s[0, 0, t] == source(row), p + 1, digit)
        which = which * (len(sources) + 1) + digit
        place = place * groups + jnp.clip(rows_s[0, 0, t], 0, groups - 1)
    plan[0] = jnp.full(plan.shape[1:], which, jnp.int32)
    plan[1] = jnp.full(plan.shape[1:], place, jnp.int32)
    for t, copy in enumerate(copies[:slots]):
        copy.wait()
        high[t], low[t] = split(held[t].T)


def split_slabs(slabs, tile_rows, tile_cols, sources, groups):
    slots = slabs.shape[0]
    outs = [pltpu.VMEM(slabs.shape, BF16)] * 2 + [pltpu.VMEM((2, SUBLANES, LANES), jnp.int32)]
    scratch = [pltpu.VMEM(slabs.shape, F32)] + [pltpu.SMEM(tile_rows.shape, jnp.int32)] * 2
    scratch.append(pltpu.SemaphoreType.DMA((slots + 2,)))
    cost = pl.CostEstimate(flops=4 * slabs.size, bytes_accessed=8 * slabs.size, transcendentals=0)
    operands = [pltpu.with_memory_space_constraint(x, pltpu.HBM) for x in (slabs, tile_rows, tile_cols)]
    kernel = functools.partial(split_kernel, sources, groups)
    return call(kernel, outs, [pl.ANY] * len(operands), "split_slabs", scratch, cost)(*operands)


def digits(number, base, count):
    return [lax.rem(lax.div(number, base ** (count - 1 - t)), base) for t in range(count)]


def product(piece, high, low):
    half_width = piece.shape[0] // 2
    by_high = dot(piece, high)
    return by_high[:half_width] + by_high[half_width:] + dot(piece[:half_width], low)


def pick(picked, t, piece):
    half_width = piece.shape[0]
    picked[t, :half_width], picked[t, half_width:] = split(piece[...])


def early_kernel(bases, counts, plan, high, low, *refs):
    pieces, (total, rest, picked, which) = refs[:-4], refs[-4:]
    slots = high.shape[0]
    place = digits(plan[1][0, 0], bases[1], slots)
    found = [jnp.where(t < counts[0, 0], d, 0) for t, d in enumerate(digits(plan[0][0, 0], bases[0], slots))]
    left = 0
    for t in range(slots):
        which[t] = found[t]
        left = left * (bases[1] + 1) + jnp.where(found[t] > len(pieces), place[t] + 1, 0)
    rest[...] = jnp.full(rest.shape, left, jnp.int32)
    for p, piece in enumerate(pieces):

        @pl.loop(0, slots)
        def _(t):
            @pl.when(which[t] == p + 1)
            def _():
                pick(picked, t, piece)

    total[...] = jnp.zeros_like(total)
    for t in range(slots):

        @pl.when((found[t] > 0) & (found[t] <= len(pieces)))
        def _():
            total[place[t]] += product(picked[t], high[t], low[t])


def late_kernel(sizes, plan, high, low, early, piece, *refs):
    groups, halves = sizes
    outs, (total, picked) = refs[:-2], refs[-2:]
    slots = high.shape[0]
    block_len = early.shape[2]
    col, rep = lax.axis_index("col"), lax.axis_index("rep")
    place = digits(plan[...][0, 0], groups + 1, slots)
    total[...] = early[...]
    pick(picked, 0, piece)
    for t in range(slots):

        @pl.when(place[t] > 0)
        def _():
            total[place[t] - 1] += product(picked[0], high[t], low[t])

    part = block_len // halves
    for i, out in enumerate(outs):
        k, h = divmod(i, halves)
        begin = pl.multiple_of(lax.rem(rep + h, halves) * part, part)
        out[...] = total[lax.rem(col + k, groups), :, pl.ds(begin, part)]


def mix(sizes, slabs, counts, plan, pieces):
    groups, halves = sizes
    slots = slabs[0].shape[0]
    half_width, block_len = pieces[0].shape
    bases = (len(pieces) + 1, groups)
    picked = pltpu.VMEM((slots, 2 * half_width, block_len), BF16)
    total, rest = call(
        functools.partial(early_kernel, bases),
        [pltpu.VMEM((groups, half_width, block_len), F32), pltpu.VMEM((SUBLANES, LANES), jnp.int32)],
        [pltpu.SMEM] + [pltpu.VMEM] * (2 + len(pieces)),
        "mix_early",
        [picked, pltpu.SMEM((slots,), jnp.int32)],
        pl.CostEstimate(flops=6 * slabs[0].size * half_width, bytes_accessed=4 * slabs[0].size, transcendentals=0),
    )(counts, plan, *slabs, *pieces[:-1])
    return call(
        functools.partial(late_kernel, sizes),
        [pltpu.VMEM((half_width, block_len // halves), F32)] * (groups * halves),
        [pltpu.VMEM] * 5,
        "mix_late",
        [pltpu.VMEM(total.shape, F32), picked],
    )(rest, *slabs, total, pieces[-1])


def node_kernel(groups, halves, *refs):
    terms, refs = refs[: groups * halves][::-1], refs[groups * halves :]
    weights, (bias, cotangent, output, *grads) = refs[:halves], refs[halves:]
    half_width = terms[0].shape[0]
    mixed = [sum(terms[k * halves + h][...] for k in range(groups)) for h in range(halves)]
    mixed = split(jnp.concatenate(mixed))
    weight = split(jnp.concatenate([w[...] for w in weights]))
    preact = bias[...] + dot_split(mixed, weight, ((0,), (0,)))
    squash = 1.0 / (1.0 + jnp.exp(-preact))
    output[...] = preact * squash
    slope = cotangent[...] * squash * (1.0 + preact * (1.0 - squash))
    bias_term = jnp.sum(slope, axis=0, keepdims=True)
    product = dot_split(mixed, split(slope), ((1,), (0,)))
    for h, grad in enumerate(grads):
        rows = product[h * half_width : (h + 1) * half_width]
        grad[:half_width] = rows.reshape(half_width, 1, rows.shape[1])
        grad[half_width] = bias_term


def node_step(sizes, terms, weights, bias, cotangent):
    groups, halves = sizes
    width = cotangent.shape[1]
    grad = pltpu.VMEM((terms[0].shape[0] + 1, 1, width), F32)
    return call(
        functools.partial(node_kernel, groups, halves),
        [pltpu.VMEM(cotangent.shape, F32)] + [grad] * halves,
        [pltpu.VMEM] * (len(terms) + halves + 2),
        "node_step",
    )(*terms[::-1], *weights, bias.reshape(1, width), cotangent)


def last_kernel(a, b, grad_weight, grad_bias):
    half_width = grad_weight.shape[0]
    total = a[...] + b[...]
    grad_weight[...] = total[:half_width].reshape(grad_weight.shape)
    grad_bias[...] = total[half_width, 0]


def last_step(a, b):
    half_width, width = a.shape[0] - 1, a.shape[2]
    out = [jax.ShapeDtypeStruct((half_width, width), F32), jax.ShapeDtypeStruct((width,), F32)]
    return call(last_kernel, out, [pltpu.VMEM] * 2, "last_step")(a, b)


def shift(x, axis, size, k):
    return lax.ppermute(x, axis, [(i, (i + k) % size) for i in range(size)])


def shift_two(x, sizes, steps):
    (groups, halves), (k, h) = sizes, steps
    perm = [
        (c * halves + r, (c + k) % groups * halves + (r + h) % halves) for c in range(groups) for r in range(halves)
    ]
    return lax.ppermute(x, ("col", "rep"), perm)


def swap(x, axis, size, bit):
    return lax.ppermute(x, axis, [(i, i ^ bit) for i in range(size)])


def swap_two(x, axes, sizes, bits):
    (_, minor), perm = sizes, []
    for i in range(sizes[0]):
        for j in range(minor):
            perm.append((i * minor + j, (i ^ bits[0]) * minor + (j ^ bits[1])))
    return lax.ppermute(x, axes, perm)


def is_power(n):
    return n & (n - 1) == 0


def line_basis(size):
    bits = [1 << i for i in range(1, size.bit_length() - 1)]
    return [size - 2] + bits[-2::-1] if bits else []


def piece_sources(size):
    if not is_power(size) or size < 2:
        return [lambda row, k=k: lax.rem(row + size - k, size) for k in range(size)]
    return [lambda row, mask=mask: lax.bitwise_xor(row, mask) for mask in piece_masks(size)]


def piece_masks(size):
    lines = [0]
    for mask in line_basis(size):
        lines += [other ^ mask for other in lines]
    last = max(lines, key=lambda mask: (lines.index(mask) > 0 and mask not in line_basis(size), lines.index(mask)))
    crossed = [mask ^ 1 for mask in lines if mask != last] + [last ^ 1]
    return lines + crossed


def gather_row(x, size, held):
    if not is_power(size) or size < 2:
        return [x] + [shift(x, "row", size, k) for k in range(1, size)], held
    basis = line_basis(size)
    own_cross = swap(x, "row", size, 1)
    pieces = {0: x, 1: own_cross}
    if len(basis) > 1:
        pieces[basis[-1] ^ 1] = swap(x, "row", size, basis[-1] ^ 1)
    lines = [0]
    for step, mask in enumerate(basis):
        for other in lines:
            if step and step == len(basis) - 1 and not other:
                free, _ = lax.optimization_barrier((x, pieces[mask ^ 1]))
                pieces[mask] = swap(free, "row", size, mask)
            else:
                pieces[other ^ mask] = swap(pieces[other], "row", size, mask)
        if step == 0:
            pieces[mask], pieces[1], held = lax.optimization_barrier((pieces[mask], pieces[1], held))
        lines += [other ^ mask for other in lines]
    order = piece_masks(size)
    for mask in lines:
        if mask ^ 1 not in pieces:
            block = pieces[mask]
            if mask ^ 1 == order[-1] and len(basis) > 1:
                block, _ = lax.optimization_barrier((block, pieces[basis[-1] ^ 1]))
            pieces[mask ^ 1] = swap(block, "row", size, 1)
    return [pieces[mask] for mask in order], held


def sum_all(grad, groups, row_size):
    if not (is_power(groups) and is_power(row_size)) or groups * row_size == 1:
        grad = lax.psum(grad, ("row", "col"))
        return grad, jnp.zeros_like(grad)
    col_bits = [1 << i for i in range(groups.bit_length() - 1)]
    row_bits = [1 << i for i in range(row_size.bit_length() - 1)]
    steps = []
    if col_bits and row_bits:
        axes, sizes, a, b = ("row", "col"), (row_size, groups), row_bits.pop(0), col_bits.pop(0)

        def square(x):
            one = swap_two(x, axes, sizes, (a, 0))
            two = swap_two(x, axes, sizes, (0, b))
            both = swap_two(x, axes, sizes, (a, b))
            return x + one, two + both

        steps.append(square)
    steps += [lambda x, bit=bit: (x, swap(x, "col", groups, bit)) for bit in col_bits]
    while row_bits:
        (one, two), row_bits = (row_bits + [0])[:2], row_bits[2:]
        if two:
            steps.append(
                lambda x, one=one, two=two: (
                    x + swap(x, "row", row_size, one ^ two),
                    swap(x, "row", row_size, two) + swap(x, "row", row_size, one),
                )
            )
        else:
            steps.append(lambda x, one=one: (x, swap(x, "row", row_size, one)))
    for step in steps[:-1]:
        terms = step(grad)
        grad = terms[0] + terms[1]
    return steps[-1](grad)


def local(row_size, groups, halves, adj_tiles, tile_rows, tile_cols, tile_counts, features_t, weight, bias_vec, cotangent):
    weights = [weight] + [shift(weight, "rep", halves, k) for k in range(1, halves)]
    *slabs, plan = split_slabs(adj_tiles[0, 0], tile_rows, tile_cols, piece_sources(row_size), groups)
    pieces, (slabs, plan, weights) = gather_row(features_t, row_size, (slabs, plan, weights))
    parts = mix((groups, halves), slabs, tile_counts, plan, pieces)

    terms = [None] * len(parts)
    for i in sorted(range(len(parts)), key=lambda i: -i):
        terms[i] = shift_two(parts[i], (groups, halves), divmod(i, halves)) if i else parts[i]
    output, *grads = node_step((groups, halves), terms, weights, bias_vec, cotangent)
    grad = grads[0]
    for k in range(1, halves):
        grad = grad + shift(grads[k], "rep", halves, -k)
    grad_weight, grad_bias = last_step(*sum_all(grad, groups, row_size))
    return output, grad_weight, grad_bias


def solution(mesh):
    row_size, groups, halves = (mesh.shape[axis] for axis in ("row", "col", "rep"))
    in_specs = (
        P("row", "col", None, None, None),
        P("row", "col", None),
        P("row", "col", None),
        P("row", "col"),
        P("rep", ("row", "col")),
        P("rep", None),
        P(),
        P(("row", "col", "rep"), None),
    )
    out_specs = (P(("row", "col", "rep"), None), P("rep", None), P())
    return jax.shard_map(
        functools.partial(local, row_size, groups, halves),
        mesh=mesh,
        in_specs=in_specs,
        out_specs=out_specs,
        check_vma=False,
    )
```

```python
import functools

import jax
import jax.numpy as jnp
from jax import lax
from jax.experimental import pallas as pl
from jax.experimental.pallas import tpu as pltpu
from jax.sharding import PartitionSpec as P

F32 = jnp.float32
BF16 = jnp.bfloat16
SUBLANES = 8
LANES = 128
VMEM_BYTES = 40 * 2**20


def dot(a, b, dims=((1,), (0,))):
    return lax.dot_general(a, b, (dims, ((), ())), preferred_element_type=F32)


def split(x):
    high = x.astype(BF16)
    return high, (x - high.astype(F32)).astype(BF16)


def dot_split(a, b, dims):
    (ah, al), (bh, bl) = a, b
    return dot(ah, bh, dims) + (dot(ah, bl, dims) + dot(al, bh, dims))


def call(kernel, out_shape, spaces, name, scratch=(), cost=None):
    return pl.pallas_call(
        kernel,
        out_shape=out_shape,
        in_specs=[pl.BlockSpec(memory_space=space) for space in spaces],
        out_specs=jax.tree.map(lambda _: pl.BlockSpec(memory_space=pltpu.VMEM), out_shape),
        scratch_shapes=list(scratch),
        compiler_params=pltpu.CompilerParams(vmem_limit_bytes=VMEM_BYTES),
        cost_estimate=cost,
        name=name,
    )


def split_kernel(sources, groups, slabs, rows, cols, high, low, plan, held, rows_s, cols_s, sems):
    slots = slabs.shape[0]
    copies = [pltpu.make_async_copy(slabs.at[t], held.at[t], sems.at[t]) for t in range(slots)]
    for k, pair in enumerate(((rows, rows_s), (cols, cols_s))):
        copies.append(pltpu.make_async_copy(*pair, sems.at[slots + k]))
    for copy in copies:
        copy.start()
    for copy in copies[slots:]:
        copy.wait()
    row = lax.axis_index("row")
    which = place = 0
    for t in range(slots):
        digit = 0
        for p, source in enumerate(sources):
            digit = jnp.where(cols_s[0, 0, t] == source(row), p + 1, digit)
        which = which * (len(sources) + 1) + digit
        place = place * groups + jnp.clip(rows_s[0, 0, t], 0, groups - 1)
    plan[0] = jnp.full(plan.shape[1:], which, jnp.int32)
    plan[1] = jnp.full(plan.shape[1:], place, jnp.int32)
    for t, copy in enumerate(copies[:slots]):
        copy.wait()
        high[t], low[t] = split(held[t].T)


def split_slabs(slabs, tile_rows, tile_cols, sources, groups):
    slots = slabs.shape[0]
    outs = [pltpu.VMEM(slabs.shape, BF16)] * 2 + [pltpu.VMEM((2, SUBLANES, LANES), jnp.int32)]
    scratch = [pltpu.VMEM(slabs.shape, F32)] + [pltpu.SMEM(tile_rows.shape, jnp.int32)] * 2
    scratch.append(pltpu.SemaphoreType.DMA((slots + 2,)))
    cost = pl.CostEstimate(flops=4 * slabs.size, bytes_accessed=8 * slabs.size, transcendentals=0)
    operands = [pltpu.with_memory_space_constraint(x, pltpu.HBM) for x in (slabs, tile_rows, tile_cols)]
    kernel = functools.partial(split_kernel, sources, groups)
    return call(kernel, outs, [pl.ANY] * len(operands), "split_slabs", scratch, cost)(*operands)


def digits(number, base, count):
    return [lax.rem(lax.div(number, base ** (count - 1 - t)), base) for t in range(count)]


def product(piece, high, low):
    half_width = piece.shape[0] // 2
    by_high = dot(piece, high)
    return by_high[:half_width] + by_high[half_width:] + dot(piece[:half_width], low)


def pick(picked, t, piece):
    half_width = piece.shape[0]
    picked[t, :half_width], picked[t, half_width:] = split(piece[...])


def live_kernel(slots, bases, counts, plan, out):
    which = digits(plan[0][0, 0], bases[0], slots)
    code = 0
    for t in range(slots):
        code = code * bases[0] + jnp.where(t < counts[0, 0], which[t], 0)
    out[0] = jnp.full(out.shape[1:], code, jnp.int32)
    out[1] = plan[1]


def live_plan(plan, counts, slots, bases):
    out = pltpu.VMEM(plan.shape, jnp.int32)
    return call(functools.partial(live_kernel, slots, bases), out, [pltpu.SMEM, pltpu.VMEM], "live_plan")(counts, plan)


def early_kernel(bases, plan, high, low, *refs):
    pieces, (total, rest, picked, which) = refs[:-4], refs[-4:]
    slots = high.shape[0]
    place = digits(plan[1][0, 0], bases[1], slots)
    found = digits(plan[0][0, 0], bases[0], slots)
    left = 0
    for t in range(slots):
        which[t] = found[t]
        left = left * (bases[1] + 1) + jnp.where(found[t] > len(pieces), place[t] + 1, 0)
    rest[...] = jnp.full(rest.shape, left, jnp.int32)
    for p, piece in enumerate(pieces):

        @pl.loop(0, slots)
        def _(t):
            @pl.when(which[t] == p + 1)
            def _():
                pick(picked, t, piece)

    total[...] = jnp.zeros_like(total)
    for t in range(slots):

        @pl.when((found[t] > 0) & (found[t] <= len(pieces)))
        def _():
            total[place[t]] += product(picked[t], high[t], low[t])


def late_kernel(sizes, plan, high, low, early, piece, *refs):
    groups, halves = sizes
    outs, (total, picked) = refs[:-2], refs[-2:]
    slots = high.shape[0]
    block_len = early.shape[2]
    col, rep = lax.axis_index("col"), lax.axis_index("rep")
    place = digits(plan[...][0, 0], groups + 1, slots)
    total[...] = early[...]
    pick(picked, 0, piece)
    for t in range(slots):

        @pl.when(place[t] > 0)
        def _():
            total[place[t] - 1] += product(picked[0], high[t], low[t])

    part = block_len // halves
    for i, out in enumerate(outs):
        k, h = divmod(i, halves)
        begin = pl.multiple_of(lax.rem(rep + h, halves) * part, part)
        out[...] = total[lax.rem(col + k, groups), :, pl.ds(begin, part)]


def mix(sizes, slabs, plan, pieces):
    groups, halves = sizes
    slots = slabs[0].shape[0]
    half_width, block_len = pieces[0].shape
    bases = (len(pieces) + 1, groups)
    picked = pltpu.VMEM((slots, 2 * half_width, block_len), BF16)
    total, rest = call(
        functools.partial(early_kernel, bases),
        [pltpu.VMEM((groups, half_width, block_len), F32), pltpu.VMEM((SUBLANES, LANES), jnp.int32)],
        [pltpu.VMEM] * (2 + len(pieces)),
        "mix_early",
        [picked, pltpu.SMEM((slots,), jnp.int32)],
        pl.CostEstimate(flops=6 * slabs[0].size * half_width, bytes_accessed=4 * slabs[0].size, transcendentals=0),
    )(plan, *slabs, *pieces[:-1])
    return call(
        functools.partial(late_kernel, sizes),
        [pltpu.VMEM((half_width, block_len // halves), F32)] * (groups * halves),
        [pltpu.VMEM] * 5,
        "mix_late",
        [pltpu.VMEM(total.shape, F32), picked],
    )(rest, *slabs, total, pieces[-1])


def node_kernel(groups, halves, *refs):
    terms, refs = refs[: groups * halves][::-1], refs[groups * halves :]
    weights, (bias, cotangent, output, *grads) = refs[:halves], refs[halves:]
    half_width = terms[0].shape[0]
    mixed = [sum(terms[k * halves + h][...] for k in range(groups)) for h in range(halves)]
    mixed = split(jnp.concatenate(mixed))
    weight = split(jnp.concatenate([w[...] for w in weights]))
    preact = bias[...] + dot_split(mixed, weight, ((0,), (0,)))
    squash = 1.0 / (1.0 + jnp.exp(-preact))
    output[...] = preact * squash
    slope = cotangent[...] * squash * (1.0 + preact * (1.0 - squash))
    bias_term = jnp.sum(slope, axis=0, keepdims=True)
    product = dot_split(mixed, split(slope), ((1,), (0,)))
    for h, grad in enumerate(grads):
        grad[:half_width] = product[h * half_width : (h + 1) * half_width]
        grad[half_width:] = jnp.broadcast_to(bias_term, (SUBLANES, bias_term.shape[1]))


def node_step(sizes, terms, weights, bias, cotangent):
    groups, halves = sizes
    width = cotangent.shape[1]
    grad = pltpu.VMEM((terms[0].shape[0] + SUBLANES, width), F32)
    return call(
        functools.partial(node_kernel, groups, halves),
        [pltpu.VMEM(cotangent.shape, F32)] + [grad] * halves,
        [pltpu.VMEM] * (len(terms) + halves + 2),
        "node_step",
    )(*terms[::-1], *weights, bias.reshape(1, width), cotangent)


def last_kernel(a, b, grad_weight, grad_bias):
    half_width = grad_weight.shape[0]
    grad_weight[...] = a[:half_width] + b[:half_width]
    grad_bias[...] = a[half_width] + b[half_width]


def last_step(a, b):
    half_width, width = a.shape[0] - SUBLANES, a.shape[1]
    out = [jax.ShapeDtypeStruct((half_width, width), F32), jax.ShapeDtypeStruct((width,), F32)]
    return call(last_kernel, out, [pltpu.VMEM] * 2, "last_step")(a, b)


def shift(x, axis, size, k):
    return lax.ppermute(x, axis, [(i, (i + k) % size) for i in range(size)])


def shift_two(x, sizes, steps):
    (groups, halves), (k, h) = sizes, steps
    perm = [
        (c * halves + r, (c + k) % groups * halves + (r + h) % halves) for c in range(groups) for r in range(halves)
    ]
    return lax.ppermute(x, ("col", "rep"), perm)


def swap(x, axis, size, bit):
    return lax.ppermute(x, axis, [(i, i ^ bit) for i in range(size)])


def swap_two(x, axes, sizes, bits):
    (_, minor), perm = sizes, []
    for i in range(sizes[0]):
        for j in range(minor):
            perm.append((i * minor + j, (i ^ bits[0]) * minor + (j ^ bits[1])))
    return lax.ppermute(x, axes, perm)


def is_power(n):
    return n & (n - 1) == 0


def line_basis(size):
    bits = [1 << i for i in range(1, size.bit_length() - 1)]
    return [size - 2] + bits[-2::-1] if bits else []


def piece_sources(size):
    if not is_power(size) or size < 2:
        return [lambda row, k=k: lax.rem(row + size - k, size) for k in range(size)]
    return [lambda row, mask=mask: lax.bitwise_xor(row, mask) for mask in piece_masks(size)]


def piece_masks(size):
    lines = [0]
    for mask in line_basis(size):
        lines += [other ^ mask for other in lines]
    last = max(lines, key=lambda mask: (lines.index(mask) > 0 and mask not in line_basis(size), lines.index(mask)))
    crossed = [mask ^ 1 for mask in lines if mask != last] + [last ^ 1]
    return lines + crossed


def gather_row(x, size, held):
    if not is_power(size) or size < 2:
        return [x] + [shift(x, "row", size, k) for k in range(1, size)], held
    basis = line_basis(size)
    own_cross = swap(x, "row", size, 1)
    pieces = {0: x, 1: own_cross}
    if len(basis) > 1:
        pieces[basis[-1] ^ 1] = swap(x, "row", size, basis[-1] ^ 1)
    lines = [0]
    for step, mask in enumerate(basis):
        for other in lines:
            if step and step == len(basis) - 1 and not other:
                free, _ = lax.optimization_barrier((x, pieces[mask ^ 1]))
                pieces[mask] = swap(free, "row", size, mask)
            else:
                pieces[other ^ mask] = swap(pieces[other], "row", size, mask)
        if step == 0:
            pieces[mask], pieces[1], held = lax.optimization_barrier((pieces[mask], pieces[1], held))
        lines += [other ^ mask for other in lines]
    order = piece_masks(size)
    for mask in lines:
        if mask ^ 1 not in pieces:
            block = pieces[mask]
            if mask ^ 1 == order[-1] and len(basis) > 1:
                block, _ = lax.optimization_barrier((block, pieces[basis[-1] ^ 1]))
            pieces[mask ^ 1] = swap(block, "row", size, 1)
    return [pieces[mask] for mask in order], held


def sum_all(grad, groups, row_size):
    if not (is_power(groups) and is_power(row_size)) or groups * row_size == 1:
        grad = lax.psum(grad, ("row", "col"))
        return grad, jnp.zeros_like(grad)
    col_bits = [1 << i for i in range(groups.bit_length() - 1)]
    row_bits = [1 << i for i in range(row_size.bit_length() - 1)]
    steps = []
    if col_bits and row_bits:
        axes, sizes, a, b = ("row", "col"), (row_size, groups), row_bits.pop(0), col_bits.pop(0)

        def square(x):
            one = swap_two(x, axes, sizes, (a, 0))
            two = swap_two(x, axes, sizes, (0, b))
            both = swap_two(x, axes, sizes, (a, b))
            return x + one, two + both

        steps.append(square)
    steps += [lambda x, bit=bit: (x, swap(x, "col", groups, bit)) for bit in col_bits]
    while row_bits:
        (one, two), row_bits = (row_bits + [0])[:2], row_bits[2:]
        if two:
            steps.append(
                lambda x, one=one, two=two: (
                    x + swap(x, "row", row_size, one ^ two),
                    swap(x, "row", row_size, two) + swap(x, "row", row_size, one),
                )
            )
        else:
            steps.append(lambda x, one=one: (x, swap(x, "row", row_size, one)))
    for step in steps[:-1]:
        terms = step(grad)
        grad = terms[0] + terms[1]
    return steps[-1](grad)


def local(row_size, groups, halves, adj_tiles, tile_rows, tile_cols, tile_counts, features_t, weight, bias_vec, cotangent):
    weights = [weight] + [shift(weight, "rep", halves, k) for k in range(1, halves)]
    *slabs, plan = split_slabs(adj_tiles[0, 0], tile_rows, tile_cols, piece_sources(row_size), groups)
    slots = tile_cols.shape[2]
    plan = live_plan(plan, tile_counts, slots, (row_size + 1, groups))
    pieces, (slabs, plan, weights) = gather_row(features_t, row_size, (slabs, plan, weights))
    parts = mix((groups, halves), slabs, plan, pieces)

    terms = [None] * len(parts)
    for i in sorted(range(len(parts)), key=lambda i: -i):
        terms[i] = shift_two(parts[i], (groups, halves), divmod(i, halves)) if i else parts[i]
    output, *grads = node_step((groups, halves), terms, weights, bias_vec, cotangent)
    grad = grads[0]
    for k in range(1, halves):
        grad = grad + shift(grads[k], "rep", halves, -k)
    grad_weight, grad_bias = last_step(*sum_all(grad, groups, row_size))
    return output, grad_weight, grad_bias


def solution(mesh):
    row_size, groups, halves = (mesh.shape[axis] for axis in ("row", "col", "rep"))
    in_specs = (
        P("row", "col", None, None, None),
        P("row", "col", None),
        P("row", "col", None),
        P("row", "col"),
        P("rep", ("row", "col")),
        P("rep", None),
        P(),
        P(("row", "col", "rep"), None),
    )
    out_specs = (P(("row", "col", "rep"), None), P("rep", None), P())
    return jax.shard_map(
        functools.partial(local, row_size, groups, halves),
        mesh=mesh,
        in_specs=in_specs,
        out_specs=out_specs,
        check_vma=False,
    )
```
